256 devices in a mesh: member: 8 (over z), space: 32 (over y, x, core).
Axes of the slice: x: 4, y: 4, z: 8, core: 2. Of those that a mesh axis runs over, the one named last changes fastest.
Arguments:
- state: bfloat16 [128, 8, 4, 256, 512], P('member', None, None, 'space'), may hold values from -6 to 6
- wind_east: float32 [8, 4, 256, 512], P(None, None, 'space'), may hold values from 0.1 to 0.45
- wind_north: float32 [8, 4, 256, 512], P(None, None, 'space'), may hold values from -0.45 to 0.45
- obs_col: int32 [32, 8, 512], P('space', 'member'), may hold values from 0 to 16383
- obs_val: float32 [32, 8, 512], P('space', 'member'), may hold values from -6 to 6
- obs_rinv: float32 [32, 8, 512], P('space', 'member'), may hold values from 0.5 to 20
- obs_count: int32 [32, 8], P('space', 'member'), may hold values from 128 to 512, as said below
- loc_class: int32 [32, 8, 3, 512], P('space', 'member'), may hold values from 0 to 3
Outputs:
- analysed: bfloat16 [128, 8, 4, 256, 512], P('member', None, None, 'space')
The draws below stay inside these ranges and needn't reach their ends.
Inputs may be any that keep to these rules, and one draw needn't show every extreme that they name: `obs_count`: a multiple of 128; some tile holds 512.
All inputs are finite; a program needn't handle non-finite values.
Results may differ from the reference program's by a relative error of at most 0.0066.
Values may be sent and summed in bfloat16 or wider, within the bound.
No kernel may reach another device: no remote copies, remote signals or barrier semaphores. Data moves between devices by JAX's collectives and lax.ppermute only.
A program may use at most 128 MiB of HBM per device.

```python
import math
import jax
import jax.numpy as jnp
from jax import lax

ENSEMBLE_SIZE = 128
MODEL_LEVELS = 4
BAND_ROW_COUNT = 8
TILE_COLUMNS = 512
NY = 256
OB = 512
BLOCK = 128
ITERS = 6
N_MEMBER = 8
N_SPACE = 32


def draw_obs_count(key, part):
    key = jax.random.fold_in(key, 7)
    first, second = jax.random.split(key)
    blocks = jax.random.randint(first, (N_SPACE, N_MEMBER), 1, OB // BLOCK + 1)
    counts = blocks * BLOCK
    chosen = jax.random.randint(second, (), 0, N_SPACE * N_MEMBER)
    places = jnp.arange(N_SPACE * N_MEMBER).reshape(N_SPACE, N_MEMBER)
    return jnp.where(places == chosen, OB, counts).astype(jnp.int32)


def place_ends(drawn, own_key, smallest, top_value):
    place = [jax.random.randint(jax.random.fold_in(own_key, axis), (), 0, length) for axis, length in enumerate(drawn.shape)]
    longest = drawn.shape.index(max(drawn.shape))
    next_to = place[:longest] + [(place[longest] + 1) % drawn.shape[longest]] + place[longest + 1:]
    return drawn.at[tuple(place)].set(smallest).at[tuple(next_to)].set(top_value)


def block_levels(key, shape, pieces, smallest, largest):
    level = 1.0
    for axis_at, shards_of in pieces:
        steps = jax.random.uniform(jax.random.fold_in(jax.random.fold_in(key, 6), axis_at), (shards_of,), jnp.float32, smallest / len(pieces), largest / len(pieces))
        level = level * jnp.repeat(jnp.exp(steps), shape[axis_at] // shards_of).reshape((-1,) + (1,) * (len(shape) - 1 - axis_at))
    return level


def normal_values(stream_key, shape, width, reach, pieces=(), kind=jnp.bfloat16):
    gain = block_levels(stream_key, shape, pieces, -0.22, 0.18) if pieces else 1.0
    array = jax.random.normal(stream_key, shape, jnp.float32) * width * gain
    return jnp.minimum(jnp.maximum(array, -reach), reach).astype(kind)


def setup_inputs(seed: int = 0) -> dict:
    key_of = jax.random.split(jax.random.key(seed), 9)
    return {
        "state": normal_values(key_of[0], (ENSEMBLE_SIZE, N_MEMBER, MODEL_LEVELS, NY, TILE_COLUMNS), 1.0, 6.0, ((0, 8), (3, 32))),
        "wind_east": jnp.clip(0.1 + 0.35 * jax.random.uniform(key_of[1], (N_MEMBER, MODEL_LEVELS, NY, TILE_COLUMNS), jnp.float32) ** block_levels(key_of[1], (N_MEMBER, MODEL_LEVELS, NY, TILE_COLUMNS), ((2, 32),), -0.2, 0.2), 0.1, 0.45),
        "wind_north": jnp.clip(jax.random.uniform(key_of[2], (N_MEMBER, MODEL_LEVELS, NY, TILE_COLUMNS), jnp.float32, -0.45, 0.45) * block_levels(key_of[2], (N_MEMBER, MODEL_LEVELS, NY, TILE_COLUMNS), ((2, 32),), -0.4, 0.0), -0.45, 0.45),
        "obs_col": place_ends(jax.random.randint(key_of[3], (N_SPACE, N_MEMBER, OB), 0, MODEL_LEVELS * BAND_ROW_COUNT * TILE_COLUMNS), jax.random.fold_in(key_of[3], 1), 0, (MODEL_LEVELS * BAND_ROW_COUNT * TILE_COLUMNS) - 1).astype(jnp.int32),
        "obs_val": normal_values(key_of[4], (N_SPACE, N_MEMBER, OB), 1.0, 6.0, ((0, 32), (1, 8)), jnp.float32),
        "obs_rinv": jnp.clip(jnp.exp(math.log(20.0) - 3.6888795 * jax.random.uniform(key_of[5], (N_SPACE, N_MEMBER, OB), jnp.float32) ** block_levels(key_of[5], (N_SPACE, N_MEMBER, OB), ((0, 32), (1, 8)), -0.2, 0.2)), 0.5, 20.0),
        "obs_count": draw_obs_count(jax.random.fold_in(key_of[8], 71), 0),
        "loc_class": place_ends(jax.random.randint(key_of[7], (N_SPACE, N_MEMBER, 3, OB), 0, 4), jax.random.fold_in(key_of[7], 1), 0, 3).astype(jnp.int32),
    }


def loc_weights(classes):
    table = (1.0, 0.55, 0.25, 0.08)
    total = jnp.zeros(classes.shape, jnp.float32)
    for index, value in enumerate(table):
        total = total + jnp.where(classes == index, jnp.float32(value), jnp.float32(0.0))
    return total

def west_of(middle):
    last = jnp.roll(middle[..., -1:], 1, axis=-4)
    return jnp.concatenate([last, middle[..., :-1]], axis=-1)

def advance(middle, south, north, wind_east, wind_north):
    west = west_of(middle)
    return middle - wind_east * (middle - west) - jnp.maximum(wind_north, 0.0) * (middle - south) - jnp.minimum(wind_north, 0.0) * (north - middle)

def make_pack(raw_values, values, rinv, count):
    ybar = lax.optimization_barrier(jnp.mean(raw_values, axis=0))
    pert = raw_values - ybar[None, :]
    innov = values - ybar
    live = jnp.arange(values.shape[0]) < count
    rlive = jnp.where(live, rinv, jnp.float32(0.0))
    return jnp.concatenate([pert, innov[None, :], rlive[None, :]], axis=0)

def tile_weights(own, south, north, classes):
    high = lax.Precision.HIGHEST
    joined = jnp.concatenate([own, south, north], axis=1)
    count_members = joined.shape[0] - 2
    pert = joined[:count_members]
    innov = joined[count_members]
    rloc = joined[count_members + 1] * loc_weights(classes.reshape(-1))
    scaled = pert * rloc[None, :]
    eye = jnp.eye(count_members, dtype=jnp.float32)
    gram = (count_members - 1.0) * eye + jnp.dot(scaled, pert.T, precision=high)
    norm = jnp.sqrt(jnp.sum(gram * gram))
    upper = gram / norm
    lower = eye
    for sweep in range(ITERS):
        factor = 1.5 * eye - 0.5 * jnp.dot(lower, upper, precision=high)
        upper = jnp.dot(upper, factor, precision=high)
        lower = jnp.dot(factor, lower, precision=high)
    drive = jnp.dot(scaled, innov, precision=high)
    wmean = jnp.dot(lower, jnp.dot(lower, drive, precision=high), precision=high) / norm
    weights = (jnp.sqrt((count_members - 1.0) / norm) * lower + wmean[:, None]).astype(jnp.bfloat16)
    colsum = lax.optimization_barrier(jnp.sum(weights.astype(jnp.float32), axis=0))
    return (weights, colsum)

def apply_weights(weights, colsum, tile_flat):
    xbar = lax.optimization_barrier(jnp.mean(tile_flat.astype(jnp.float32), axis=0))
    mixed = jnp.dot(weights.T, tile_flat, preferred_element_type=jnp.float32)
    return (xbar[None, :] * (1.0 - colsum)[:, None] + mixed).astype(jnp.bfloat16)

def step_whole(field, wind_east, wind_north):
    zeros = jnp.zeros_like(field[:, :, :1])
    south = jnp.concatenate([zeros, field[:, :, :-1]], axis=2)
    north = jnp.concatenate([field[:, :, 1:], zeros], axis=2)
    return advance(field, south, north, wind_east, wind_north)

def reference(state, wind_east, wind_north, obs_col, obs_val, obs_rinv, obs_count, loc_class):

    def predict_member(single_member_state):
        field = single_member_state.astype(jnp.float32)
        field = step_whole(field, wind_east, wind_north)
        field = step_whole(field, wind_east, wind_north)
        return field.astype(jnp.bfloat16)
    predict_state = lax.map(predict_member, state)
    split_into_tiles = predict_state.reshape(ENSEMBLE_SIZE, N_MEMBER, MODEL_LEVELS, N_SPACE, BAND_ROW_COUNT, TILE_COLUMNS)
    ntiles = N_SPACE * N_MEMBER

    def get_tile(index):
        band = (index // N_MEMBER).astype(jnp.int32)
        slot = (index % N_MEMBER).astype(jnp.int32)
        zero = jnp.zeros((), jnp.int32)
        piece = lax.dynamic_slice(split_into_tiles, (zero, slot, zero, band, zero, zero), (ENSEMBLE_SIZE, 1, MODEL_LEVELS, 1, BAND_ROW_COUNT, TILE_COLUMNS))
        return piece.reshape(ENSEMBLE_SIZE, MODEL_LEVELS * BAND_ROW_COUNT * TILE_COLUMNS)

    def pack_one(items):
        index, columns, values, rinv, count = items
        tile_flat = get_tile(index)
        raw_values = jnp.take(tile_flat, columns, axis=1).astype(jnp.float32)
        return make_pack(raw_values, values, rinv, count)
    indices = jnp.arange(ntiles, dtype=jnp.int32)
    packs = lax.map(pack_one, (indices, obs_col.reshape(ntiles, OB), obs_val.reshape(ntiles, OB), obs_rinv.reshape(ntiles, OB), obs_count.reshape(ntiles)))
    packs = packs.reshape(N_SPACE, N_MEMBER, ENSEMBLE_SIZE + 2, OB)
    padded = jnp.pad(packs, ((1, 1), (0, 0), (0, 0), (0, 0)))

    def analyse_one(items):
        index, classes = items
        band = index // N_MEMBER
        slot = index % N_MEMBER
        own = packs[band, slot]
        south = padded[band, slot]
        north = padded[band + 2, slot]
        weights, colsum = tile_weights(own, south, north, classes)
        return apply_weights(weights, colsum, get_tile(index))
    result = lax.map(analyse_one, (indices, loc_class.reshape(ntiles, 3, OB)))
    result = result.reshape(N_SPACE, N_MEMBER, ENSEMBLE_SIZE, MODEL_LEVELS, BAND_ROW_COUNT, TILE_COLUMNS)
    result = jnp.transpose(result, (2, 1, 3, 0, 4, 5))
    return result.reshape(ENSEMBLE_SIZE, N_MEMBER, MODEL_LEVELS, NY, TILE_COLUMNS)
```

```python
import functools

import jax
import jax.numpy as jnp
from jax import lax
from jax.experimental import pallas as pl
from jax.experimental.pallas import tpu as pltpu
from jax.sharding import PartitionSpec as P

ITERS = 6
LANES = 128
VMEM_LIMIT = 48 * 1024 * 1024


def params(limit=VMEM_LIMIT):
    return pltpu.CompilerParams(vmem_limit_bytes=limit)


def cost(micros):
    return pl.CostEstimate(flops=0, bytes_accessed=int(micros * 3.6e6), transcendentals=0)


def order_rows(shape, members, rows):
    at = lax.broadcasted_iota(jnp.int32, shape, 0)
    source = lax.broadcasted_iota(jnp.int32, shape, 1)
    slot = at // members
    row = jnp.zeros(shape, jnp.int32)
    for index, value in enumerate(rows):
        row = jnp.where(slot == index, value, row)
    band = 8
    return jnp.where(source == (at % members) * band + row, 1.0, 0.0).astype(jnp.bfloat16)


def tile_rows(state_ref, tile, order):
    block = state_ref[:, tile, 0].astype(jnp.float32)
    members, rows, width = block.shape
    flat = block.reshape(members * rows, width).astype(jnp.bfloat16)
    return jnp.dot(order, flat, preferred_element_type=jnp.float32)


def edges_kernel(state_ref, low_ref, high_ref):
    members, tiles, _, rows, width = state_ref.shape
    order = order_rows((4 * members, members * rows), members, (0, 1, rows - 2, rows - 1))
    for tile in range(tiles):
        moved = tile_rows(state_ref, tile, order).astype(jnp.bfloat16)
        columns = slice(tile * width, (tile + 1) * width)
        for row in range(2):
            low_ref[0, row, :, columns] = moved[row * members : (row + 1) * members]
            high_ref[0, row, :, columns] = moved[(row + 2) * members : (row + 3) * members]


def edge_rows(state):
    members, tiles, levels, rows, width = state.shape
    shape = (levels, 2, members, tiles * width)
    block = pl.BlockSpec((1, 2, members, tiles * width), lambda i: (i, 0, 0, 0))
    return pl.pallas_call(
        edges_kernel,
        grid=(levels,),
        in_specs=[pl.BlockSpec((members, tiles, 1, rows, width), lambda i: (0, 0, i, 0, 0))],
        out_specs=[block, block],
        out_shape=[jax.ShapeDtypeStruct(shape, jnp.bfloat16)] * 2,
        compiler_params=params(),
        cost_estimate=cost(3),
        name="edges",
    )(state)


def step_rows(field, made, coef, tiles, width, rows_out, first_row):
    for row in rows_out:
        at = row - first_row
        for tile in range(tiles):
            columns = slice(LANES + tile * width, LANES + (tile + 1) * width)
            padded = slice(tile * width, LANES + (tile + 1) * width)
            west = pltpu.roll(field[at, :, padded], 1, 1)[:, LANES:]
            stay = coef[0, tile, at : at + 1, :]
            east = coef[1, tile, at : at + 1, :]
            up = coef[2, tile, at : at + 1, :]
            down = coef[3, tile, at : at + 1, :]
            made[at, :, columns] = (
                stay * field[at, :, columns]
                + east * west
                + up * field[at - 1, :, columns]
                + down * field[at + 1, :, columns]
            )
        made[at, :, 0:LANES] = made[at, :, tiles * width : tiles * width + LANES]


def set_coef(coef, slots, tile, east, north):
    up = jnp.maximum(north, 0.0)
    down = -jnp.minimum(north, 0.0)
    coef[0, tile, slots, :] = 1.0 - east - up - down
    coef[1, tile, slots, :] = east
    coef[2, tile, slots, :] = up
    coef[3, tile, slots, :] = down


def interior_kernel(state_ref, east_ref, north_ref, out_ref, field, made, coef):
    members, tiles, _, rows, width = state_ref.shape
    order = order_rows((rows * members, members * rows), members, tuple(range(rows)))
    for tile in range(tiles):
        moved = tile_rows(state_ref, tile, order)
        columns = slice(LANES + tile * width, LANES + (tile + 1) * width)
        for row in range(rows):
            field[row, :, columns] = moved[row * members : (row + 1) * members]
        set_coef(coef, slice(0, rows), tile, east_ref[tile, 0], north_ref[tile, 0])
    for row in range(rows):
        field[row, :, 0:LANES] = field[row, :, tiles * width : tiles * width + LANES]
    step_rows(field, made, coef, tiles, width, range(1, rows - 1), 0)
    step_rows(made, field, coef, tiles, width, range(2, rows - 2), 0)
    for row in range(2, rows - 2):
        for tile in range(tiles):
            columns = slice(LANES + tile * width, LANES + (tile + 1) * width)
            kept = slice((row - 2) * width, (row - 1) * width)
            out_ref[tile, :, kept] = field[row, :, columns].astype(jnp.bfloat16)


def interior(state, wind_east, wind_north):
    members, tiles, levels, rows, width = state.shape
    wind = pl.BlockSpec((tiles, 1, rows, width), lambda i: (0, i, 0, 0))
    part = (rows - 4) * width
    return pl.pallas_call(
        interior_kernel,
        grid=(levels,),
        in_specs=[pl.BlockSpec((members, tiles, 1, rows, width), lambda i: (0, 0, i, 0, 0)), wind, wind],
        out_specs=pl.BlockSpec((tiles, members, part), lambda i: (0, 0, i)),
        out_shape=jax.ShapeDtypeStruct((tiles, members, levels * part), jnp.bfloat16),
        scratch_shapes=[
            pltpu.VMEM((rows, members, LANES + tiles * width), jnp.float32),
            pltpu.VMEM((rows, members, LANES + tiles * width), jnp.float32),
            pltpu.VMEM((4, tiles, rows, width), jnp.float32),
        ],
        compiler_params=params(),
        cost_estimate=cost(8),
        name="interior",
    )(state, wind_east, wind_north)


def outer_kernel(
    state_ref, east_ref, north_ref, below_ref, above_ref, wind_below_ref, wind_above_ref, out_ref, field, made, coef
):
    members, tiles, _, rows, width = state_ref.shape
    order = order_rows((rows * members, members * rows), members, tuple(range(rows)))
    for tile in range(tiles):
        moved = tile_rows(state_ref, tile, order)
        columns = slice(LANES + tile * width, LANES + (tile + 1) * width)
        for row in range(rows):
            field[row + 2, :, columns] = moved[row * members : (row + 1) * members]
        set_coef(coef, slice(2, rows + 2), tile, east_ref[tile, 0], north_ref[tile, 0])
        for slot, wind_ref in ((1, wind_below_ref), (rows + 2, wind_above_ref)):
            set_coef(
                coef,
                slice(slot, slot + 1),
                tile,
                wind_ref[0, 0, tile : tile + 1, :],
                wind_ref[1, 0, tile : tile + 1, :],
            )
    for row in range(2):
        field[row, :, LANES:] = below_ref[0, row].astype(jnp.float32)
        field[rows + 2 + row, :, LANES:] = above_ref[0, row].astype(jnp.float32)
    for slot in range(rows + 4):
        field[slot, :, 0:LANES] = field[slot, :, tiles * width : tiles * width + LANES]
    step_rows(field, made, coef, tiles, width, (-1, 0, 1, 2, rows - 3, rows - 2, rows - 1, rows), -2)
    step_rows(made, field, coef, tiles, width, (0, 1, rows - 2, rows - 1), -2)
    for index, row in enumerate((0, 1, rows - 2, rows - 1)):
        for tile in range(tiles):
            columns = slice(LANES + tile * width, LANES + (tile + 1) * width)
            kept = slice(index * width, (index + 1) * width)
            out_ref[tile, :, kept] = field[row + 2, :, columns].astype(jnp.bfloat16)


def outer(state, wind_east, wind_north, below, above, wind_below, wind_above):
    members, tiles, levels, rows, width = state.shape
    wind = pl.BlockSpec((tiles, 1, rows, width), lambda i: (0, i, 0, 0))
    edge = pl.BlockSpec((1, 2, members, tiles * width), lambda i: (i, 0, 0, 0))
    wind_edge = pl.BlockSpec((2, 1, tiles, width), lambda i: (0, i, 0, 0))
    part = 4 * width
    return pl.pallas_call(
        outer_kernel,
        grid=(levels,),
        in_specs=[
            pl.BlockSpec((members, tiles, 1, rows, width), lambda i: (0, 0, i, 0, 0)),
            wind,
            wind,
            edge,
            edge,
            wind_edge,
            wind_edge,
        ],
        out_specs=pl.BlockSpec((tiles, members, part), lambda i: (0, 0, i)),
        out_shape=jax.ShapeDtypeStruct((tiles, members, levels * part), jnp.bfloat16),
        scratch_shapes=[
            pltpu.VMEM((rows + 4, members, LANES + tiles * width), jnp.float32),
            pltpu.VMEM((rows + 4, members, LANES + tiles * width), jnp.float32),
            pltpu.VMEM((4, tiles, rows + 4, width), jnp.float32),
        ],
        compiler_params=params(),
        cost_estimate=cost(9),
        name="outer",
    )(state, wind_east, wind_north, below, above, wind_below, wind_above)


def pick_kernel(place_ref, shift_ref, inner_ref, outer_ref, raw_ref, pieces):
    tile = pl.program_id(0)
    members, length = inner_ref.shape[1:]
    count = length // LANES
    for piece in range(count):
        lanes = slice(piece * LANES, (piece + 1) * LANES)
        pieces[piece] = inner_ref[0, :, lanes].astype(jnp.float32)
        pieces[count + piece] = outer_ref[0, :, lanes].astype(jnp.float32)
    lane = lax.broadcasted_iota(jnp.int32, (members, LANES), 1)
    unroll = 16
    for block in range(raw_ref.shape[2] // LANES):

        def body(step, total):
            for inside in range(unroll):
                slot = step * unroll + inside
                at = block * LANES + slot
                rolled = pltpu.roll(pieces[place_ref[tile, at]], shift_ref[tile, at], 1)
                total = jnp.where(lane == slot, rolled, total)
            return total

        total = lax.fori_loop(0, LANES // unroll, body, jnp.zeros((members, LANES), jnp.float32))
        raw_ref[0, :, block * LANES : (block + 1) * LANES] = total.astype(jnp.bfloat16)


def pick(place, shift, inner, outer_part):
    tiles, members, length = inner.shape
    slots = place.shape[1]
    half = pl.BlockSpec((1, members, length), lambda i, *_: (i, 0, 0))
    return pl.pallas_call(
        pick_kernel,
        grid_spec=pltpu.PrefetchScalarGridSpec(
            num_scalar_prefetch=2,
            grid=(tiles,),
            in_specs=[half, half],
            out_specs=pl.BlockSpec((1, members, slots), lambda i, *_: (i, 0, 0)),
            scratch_shapes=[pltpu.VMEM((2 * length // LANES, members, LANES), jnp.float32)],
        ),
        out_shape=jax.ShapeDtypeStruct((tiles, members, slots), jnp.bfloat16),
        compiler_params=params(),
        cost_estimate=cost(15),
        name="pick",
    )(place, shift, inner, outer_part)


def loc_weights(classes):
    table = (1.0, 0.55, 0.25, 0.08)
    total = jnp.zeros(classes.shape, jnp.float32)
    for index, value in enumerate(table):
        total = total + jnp.where(classes == index, jnp.float32(value), jnp.float32(0.0))
    return total


def weights_kernel(own_ref, south_ref, north_ref, obs_ref, class_ref, mix_ref, rest_ref):
    dot = functools.partial(jnp.dot, precision=lax.Precision.HIGHEST, preferred_element_type=jnp.float32)
    members = own_ref.shape[0]
    row = lax.broadcasted_iota(jnp.int32, (members, members), 0)
    column = lax.broadcasted_iota(jnp.int32, (members, members), 1)
    eye = jnp.where(row == column, 1.0, 0.0).astype(jnp.float32)
    gram = (members - 1.0) * eye
    drive = jnp.zeros((members, 1), jnp.float32)
    for index, raw_ref in enumerate((own_ref, south_ref, north_ref)):
        raw = raw_ref[...].astype(jnp.float32)
        ybar = jnp.sum(raw, axis=0, keepdims=True) * (1.0 / members)
        pert = raw - ybar
        innov = obs_ref[index, 0:1, :] - ybar
        rloc = obs_ref[index, 1:2, :] * loc_weights(class_ref[index : index + 1, :])
        scaled = pert * rloc
        gram = gram + lax.dot_general(
            scaled,
            pert,
            (((1,), (1,)), ((), ())),
            precision=lax.Precision.HIGHEST,
            preferred_element_type=jnp.float32,
        )
        drive = drive + jnp.sum(scaled * innov, axis=1, keepdims=True)
    norm = jnp.sqrt(jnp.sum(jnp.sum(gram * gram, axis=1, keepdims=True), axis=0, keepdims=True))
    upper = gram / norm
    lower = eye
    for sweep in range(ITERS):
        factor = 1.5 * eye - 0.5 * dot(lower, upper)
        if sweep < ITERS - 1:
            upper = dot(upper, factor)
        lower = dot(factor, lower)
    wide = jnp.broadcast_to(drive, (members, members))
    wmean = dot(lower, dot(lower, wide)) / norm
    weights = (jnp.sqrt((members - 1.0) / norm) * lower + wmean).astype(jnp.bfloat16).astype(jnp.float32)
    turned = weights.T
    rest = 1.0 - jnp.sum(turned, axis=1, keepdims=True)
    rows = 8
    rest_ref[...] = jnp.broadcast_to(rest[:, :, None], (members, rows, LANES)).reshape(members * rows, LANES)
    spread = jnp.broadcast_to(turned[:, None, :], (members, rows, members)).reshape(members * rows, members)
    held = lax.broadcasted_iota(jnp.int32, (members * rows, members), 0) % rows
    for index, value in enumerate((2, 3, 4, 5, 0, 1, 6, 7)):
        mix_ref[:, index * members : (index + 1) * members] = jnp.where(held == value, spread, 0.0).astype(jnp.bfloat16)


def tile_mix(own, south, north, obs, classes):
    members = own.shape[0]
    return pl.pallas_call(
        weights_kernel,
        out_shape=[
            jax.ShapeDtypeStruct((members * 8, members * 8), jnp.bfloat16),
            jax.ShapeDtypeStruct((members * 8, LANES), jnp.float32),
        ],
        compiler_params=params(),
        cost_estimate=cost(12),
        name="weights",
    )(own, south, north, obs, classes)


def mix_kernel(mix_ref, rest_ref, inner_ref, outer_ref, out_ref):
    groups, each, part = inner_ref.shape
    members = groups * each
    width = part // 4
    inner = inner_ref[...].reshape(members, part)
    outer_part = outer_ref[...].reshape(members, part)
    pieces = [inner[:, i * width : (i + 1) * width] for i in range(4)]
    pieces += [outer_part[:, i * width : (i + 1) * width] for i in range(4)]
    stacked = jnp.concatenate(pieces, axis=0)
    rows = 8
    at = lax.broadcasted_iota(jnp.int32, (rows, members * rows), 0)
    slot = lax.broadcasted_iota(jnp.int32, (rows, members * rows), 1) // members
    source = jnp.zeros((rows, members * rows), jnp.int32)
    for index, value in enumerate((2, 3, 4, 5, 0, 1, 6, 7)):
        source = jnp.where(slot == index, value, source)
    ones = jnp.where(at == source, 1.0, 0.0).astype(jnp.bfloat16)
    mean = jnp.dot(ones, stacked, preferred_element_type=jnp.float32) * (1.0 / members)
    mixed = jnp.dot(mix_ref[...], stacked, preferred_element_type=jnp.float32)
    for index in range(width // LANES):
        lanes = slice(index * LANES, (index + 1) * LANES)
        rest = rest_ref[...].reshape(members, rows, LANES)
        made = mixed[:, lanes].reshape(members, rows, LANES) + mean[None, :, lanes] * rest
        out_ref[:, :, 0, :, lanes] = made.reshape(groups, each, rows, LANES).astype(jnp.bfloat16)


def analyse(mix, rest, inner, outer_part, levels, width):
    groups, each, _ = inner.shape
    half = pl.BlockSpec((groups, each, 4 * width), lambda i: (0, 0, i))
    return pl.pallas_call(
        mix_kernel,
        grid=(levels,),
        in_specs=[
            pl.BlockSpec(mix.shape, lambda i: (0, 0)),
            pl.BlockSpec(rest.shape, lambda i: (0, 0)),
            half,
            half,
        ],
        out_specs=pl.BlockSpec((groups, each, 1, 8, width), lambda i: (0, 0, i, 0, 0)),
        out_shape=jax.ShapeDtypeStruct((groups, each, levels, 8, width), jnp.bfloat16),
        compiler_params=params(),
        cost_estimate=cost(6),
        name="analyse",
    )(mix, rest, inner, outer_part)


def to_neighbours(low, high):
    devices = lax.axis_size("space")
    up = [(i, i + 1) for i in range(devices - 1)]
    down = [(i + 1, i) for i in range(devices - 1)]
    return lax.ppermute(high, "space", up), lax.ppermute(low, "space", down)


def swap_members(blocks):
    devices = lax.axis_size("member")
    here = lax.axis_index("member")
    got = [lax.dynamic_index_in_dim(blocks, here, 0, keepdims=False)]
    for shift in range(1, devices):
        block = lax.dynamic_index_in_dim(blocks, lax.rem(here + shift, devices), 0, keepdims=False)
        got.append(lax.ppermute(block, "member", [(i, (i + shift) % devices) for i in range(devices)]))
    stacked = jnp.stack(got)
    out = jnp.zeros_like(blocks)
    for shift in range(devices):
        out = lax.dynamic_update_index_in_dim(out, got[shift], lax.rem(here + devices - shift, devices), 0)
    return out


def all_to_all(blocks):
    return lax.all_to_all(blocks, "member", split_axis=0, concat_axis=0, tiled=True)


def on_device(state, wind_east, wind_north, obs_col, obs_val, obs_rinv, obs_count, loc_class):
    members, tiles, levels, rows, width = state.shape
    slots = obs_col.shape[2]

    low, high = edge_rows(state)
    below, above = to_neighbours(low, high)
    winds = jnp.stack([wind_east[:, :, 0], wind_north[:, :, 0], wind_east[:, :, rows - 1], wind_north[:, :, rows - 1]])
    winds = jnp.swapaxes(winds, 1, 2)
    wind_below, wind_above = to_neighbours(winds[0:2], winds[2:4])

    live = jnp.arange(slots, dtype=jnp.int32) < obs_count[0, 0]
    obs = jnp.stack([obs_val[0, 0], jnp.where(live, obs_rinv[0, 0], jnp.float32(0.0))])
    obs_south, obs_north = to_neighbours(obs, obs)

    columns = lax.all_gather(obs_col[0, 0], "member")
    row = (columns // width) % rows
    inside = (row >= 2) & (row < rows - 2)
    kept = jnp.where(inside, row - 2, jnp.where(row < 2, row, row - 4))
    offset = (columns // (rows * width)) * (4 * width) + kept * width + columns % width
    place = offset // LANES + jnp.where(inside, 0, levels * 4 * width // LANES)
    shift = (jnp.arange(slots, dtype=jnp.int32)[None, :] - offset) % LANES

    inner = interior(state, wind_east, wind_north)
    inner_tile = all_to_all(inner)
    outside = outer(state, wind_east, wind_north, below, above, wind_below, wind_above)
    raw = swap_members(pick(place, shift, inner, outside)).reshape(tiles * members, slots)
    south, north = to_neighbours(raw, raw)
    mix, rest = tile_mix(raw, south, north, jnp.stack([obs, obs_south, obs_north]), loc_class[0, 0])
    outer_tile = all_to_all(outside)
    updated = analyse(mix, rest, inner_tile, outer_tile, levels, width)
    final = all_to_all(updated)
    return jnp.swapaxes(final, 0, 1)


def solution(mesh):
    return jax.shard_map(
        on_device,
        mesh=mesh,
        in_specs=(
            P("member", None, None, "space", None),
            P(None, None, "space", None),
            P(None, None, "space", None),
            P("space", "member", None),
            P("space", "member", None),
            P("space", "member", None),
            P("space", "member"),
            P("space", "member", None, None),
        ),
        out_specs=P("member", None, None, "space", None),
        check_vma=False,
    )
```

```python
import functools

import jax
import jax.numpy as jnp
from jax import lax
from jax.experimental import pallas as pl
from jax.experimental.pallas import tpu as pltpu
from jax.sharding import PartitionSpec as P

ITERS = 6
LANES = 128
VMEM_LIMIT = 48 * 1024 * 1024


def params(limit=VMEM_LIMIT):
    return pltpu.CompilerParams(vmem_limit_bytes=limit)


def cost(micros):
    return pl.CostEstimate(flops=0, bytes_accessed=int(micros * 3.6e6), transcendentals=0)


def order_rows(shape, members, rows):
    at = lax.broadcasted_iota(jnp.int32, shape, 0)
    source = lax.broadcasted_iota(jnp.int32, shape, 1)
    slot = at // members
    row = jnp.zeros(shape, jnp.int32)
    for index, value in enumerate(rows):
        row = jnp.where(slot == index, value, row)
    band = 8
    return jnp.where(source == (at % members) * band + row, 1.0, 0.0).astype(jnp.bfloat16)


def tile_rows(state_ref, tile, order):
    block = state_ref[:, tile, 0].astype(jnp.float32)
    members, rows, width = block.shape
    flat = block.reshape(members * rows, width).astype(jnp.bfloat16)
    return jnp.dot(order, flat, preferred_element_type=jnp.float32)


def edges_kernel(state_ref, low_ref, high_ref):
    members, tiles, _, rows, width = state_ref.shape
    order = order_rows((4 * members, members * rows), members, (0, 1, rows - 2, rows - 1))
    for tile in range(tiles):
        moved = tile_rows(state_ref, tile, order).astype(jnp.bfloat16)
        columns = slice(tile * width, (tile + 1) * width)
        for row in range(2):
            low_ref[0, row, :, columns] = moved[row * members : (row + 1) * members]
            high_ref[0, row, :, columns] = moved[(row + 2) * members : (row + 3) * members]


def edge_rows(state):
    members, tiles, levels, rows, width = state.shape
    shape = (levels, 2, members, tiles * width)
    block = pl.BlockSpec((1, 2, members, tiles * width), lambda i: (i, 0, 0, 0))
    return pl.pallas_call(
        edges_kernel,
        grid=(levels,),
        in_specs=[pl.BlockSpec((members, tiles, 1, rows, width), lambda i: (0, 0, i, 0, 0))],
        out_specs=[block, block],
        out_shape=[jax.ShapeDtypeStruct(shape, jnp.bfloat16)] * 2,
        compiler_params=params(),
        cost_estimate=cost(3),
        name="edges",
    )(state)


def step_rows(field, made, coef, tiles, width, rows_out, first_row):
    for row in rows_out:
        at = row - first_row
        for tile in range(tiles):
            columns = slice(LANES + tile * width, LANES + (tile + 1) * width)
            padded = slice(tile * width, LANES + (tile + 1) * width)
            west = pltpu.roll(field[at, :, padded], 1, 1)[:, LANES:]
            stay = coef[0, tile, at : at + 1, :]
            east = coef[1, tile, at : at + 1, :]
            up = coef[2, tile, at : at + 1, :]
            down = coef[3, tile, at : at + 1, :]
            made[at, :, columns] = (
                stay * field[at, :, columns]
                + east * west
                + up * field[at - 1, :, columns]
                + down * field[at + 1, :, columns]
            )
        made[at, :, 0:LANES] = made[at, :, tiles * width : tiles * width + LANES]


def set_coef(coef, slots, tile, east, north):
    up = jnp.maximum(north, 0.0)
    down = -jnp.minimum(north, 0.0)
    coef[0, tile, slots, :] = 1.0 - east - up - down
    coef[1, tile, slots, :] = east
    coef[2, tile, slots, :] = up
    coef[3, tile, slots, :] = down


def interior_kernel(state_ref, east_ref, north_ref, out_ref, field, made, coef):
    members, tiles, _, rows, width = state_ref.shape
    order = order_rows((rows * members, members * rows), members, tuple(range(rows)))
    for tile in range(tiles):
        moved = tile_rows(state_ref, tile, order)
        columns = slice(LANES + tile * width, LANES + (tile + 1) * width)
        for row in range(rows):
            field[row, :, columns] = moved[row * members : (row + 1) * members]
        set_coef(coef, slice(0, rows), tile, east_ref[tile, 0], north_ref[tile, 0])
    for row in range(rows):
        field[row, :, 0:LANES] = field[row, :, tiles * width : tiles * width + LANES]
    step_rows(field, made, coef, tiles, width, range(1, rows - 1), 0)
    step_rows(made, field, coef, tiles, width, range(2, rows - 2), 0)
    for row in range(2, rows - 2):
        for tile in range(tiles):
            columns = slice(LANES + tile * width, LANES + (tile + 1) * width)
            kept = slice((row - 2) * width, (row - 1) * width)
            out_ref[tile, :, kept] = field[row, :, columns].astype(jnp.bfloat16)


def interior(state, wind_east, wind_north):
    members, tiles, levels, rows, width = state.shape
    wind = pl.BlockSpec((tiles, 1, rows, width), lambda i: (0, i, 0, 0))
    part = (rows - 4) * width
    return pl.pallas_call(
        interior_kernel,
        grid=(levels,),
        in_specs=[pl.BlockSpec((members, tiles, 1, rows, width), lambda i: (0, 0, i, 0, 0)), wind, wind],
        out_specs=pl.BlockSpec((tiles, members, part), lambda i: (0, 0, i)),
        out_shape=jax.ShapeDtypeStruct((tiles, members, levels * part), jnp.bfloat16),
        scratch_shapes=[
            pltpu.VMEM((rows, members, LANES + tiles * width), jnp.float32),
            pltpu.VMEM((rows, members, LANES + tiles * width), jnp.float32),
            pltpu.VMEM((4, tiles, rows, width), jnp.float32),
        ],
        compiler_params=params(60 * 1024 * 1024),
        cost_estimate=cost(8),
        name="interior",
    )(state, wind_east, wind_north)


def outer_kernel(
    state_ref, east_ref, north_ref, below_ref, above_ref, wind_below_ref, wind_above_ref, out_ref, field, made, coef
):
    members, tiles, _, rows, width = state_ref.shape
    order = order_rows((rows * members, members * rows), members, tuple(range(rows)))
    for tile in range(tiles):
        moved = tile_rows(state_ref, tile, order)
        columns = slice(LANES + tile * width, LANES + (tile + 1) * width)
        for row in range(rows):
            field[row + 2, :, columns] = moved[row * members : (row + 1) * members]
        set_coef(coef, slice(2, rows + 2), tile, east_ref[tile, 0], north_ref[tile, 0])
        for slot, wind_ref in ((1, wind_below_ref), (rows + 2, wind_above_ref)):
            set_coef(
                coef,
                slice(slot, slot + 1),
                tile,
                wind_ref[0, 0, tile : tile + 1, :],
                wind_ref[1, 0, tile : tile + 1, :],
            )
    for row in range(2):
        field[row, :, LANES:] = below_ref[0, row].astype(jnp.float32)
        field[rows + 2 + row, :, LANES:] = above_ref[0, row].astype(jnp.float32)
    for slot in range(rows + 4):
        field[slot, :, 0:LANES] = field[slot, :, tiles * width : tiles * width + LANES]
    step_rows(field, made, coef, tiles, width, (-1, 0, 1, 2, rows - 3, rows - 2, rows - 1, rows), -2)
    step_rows(made, field, coef, tiles, width, (0, 1, rows - 2, rows - 1), -2)
    for index, row in enumerate((0, 1, rows - 2, rows - 1)):
        for tile in range(tiles):
            columns = slice(LANES + tile * width, LANES + (tile + 1) * width)
            kept = slice(index * width, (index + 1) * width)
            out_ref[tile, :, kept] = field[row + 2, :, columns].astype(jnp.bfloat16)


def outer(state, wind_east, wind_north, below, above, wind_below, wind_above):
    members, tiles, levels, rows, width = state.shape
    wind = pl.BlockSpec((tiles, 1, rows, width), lambda i: (0, i, 0, 0))
    edge = pl.BlockSpec((1, 2, members, tiles * width), lambda i: (i, 0, 0, 0))
    wind_edge = pl.BlockSpec((2, 1, tiles, width), lambda i: (0, i, 0, 0))
    part = 4 * width
    return pl.pallas_call(
        outer_kernel,
        grid=(levels,),
        in_specs=[
            pl.BlockSpec((members, tiles, 1, rows, width), lambda i: (0, 0, i, 0, 0)),
            wind,
            wind,
            edge,
            edge,
            wind_edge,
            wind_edge,
        ],
        out_specs=pl.BlockSpec((tiles, members, part), lambda i: (0, 0, i)),
        out_shape=jax.ShapeDtypeStruct((tiles, members, levels * part), jnp.bfloat16),
        scratch_shapes=[
            pltpu.VMEM((rows + 4, members, LANES + tiles * width), jnp.float32),
            pltpu.VMEM((rows + 4, members, LANES + tiles * width), jnp.float32),
            pltpu.VMEM((4, tiles, rows + 4, width), jnp.float32),
        ],
        compiler_params=params(),
        cost_estimate=cost(9),
        name="outer",
    )(state, wind_east, wind_north, below, above, wind_below, wind_above)


def pick_kernel(place_ref, lane_ref, inner_ref, outer_ref, raw_ref):
    members, length = inner_ref.shape[1:]
    slots = raw_ref.shape[2]
    count = length // LANES
    at_lane = lax.broadcasted_iota(jnp.int32, (LANES, slots), 0)
    chosen = jnp.where(at_lane == lane_ref[0], 1.0, 0.0).astype(jnp.bfloat16)
    place = jnp.broadcast_to(place_ref[0], (members, slots))
    total = jnp.zeros((members, slots), jnp.float32)
    together = LANES // members
    for index, half_ref in enumerate((inner_ref, outer_ref)):
        for first in range(0, count, together):
            pieces = [half_ref[0, :, (first + i) * LANES : (first + i + 1) * LANES] for i in range(together)]
            found = jnp.dot(jnp.concatenate(pieces, axis=0), chosen, preferred_element_type=jnp.float32)
            for i in range(together):
                here = place == index * count + first + i
                total = jnp.where(here, found[i * members : (i + 1) * members], total)
    raw_ref[0] = total.astype(jnp.bfloat16)


def pick(place, lane, inner, outer_part):
    tiles, members, length = inner.shape
    slots = place.shape[2]
    half = pl.BlockSpec((1, members, length), lambda i: (i, 0, 0))
    one = pl.BlockSpec((1, 1, slots), lambda i: (i, 0, 0))
    return pl.pallas_call(
        pick_kernel,
        grid=(tiles,),
        in_specs=[one, one, half, half],
        out_specs=pl.BlockSpec((1, members, slots), lambda i: (i, 0, 0)),
        out_shape=jax.ShapeDtypeStruct((tiles, members, slots), jnp.bfloat16),
        compiler_params=params(),
        cost_estimate=cost(8),
        name="pick",
    )(place, lane, inner, outer_part)


def loc_weights(classes):
    table = (1.0, 0.55, 0.25, 0.08)
    total = jnp.zeros(classes.shape, jnp.float32)
    for index, value in enumerate(table):
        total = total + jnp.where(classes == index, jnp.float32(value), jnp.float32(0.0))
    return total


def weights_kernel(own_ref, south_ref, north_ref, obs_ref, class_ref, mix_ref, rest_ref):
    dot = functools.partial(jnp.dot, precision=lax.Precision.HIGHEST, preferred_element_type=jnp.float32)
    members = own_ref.shape[0]
    row = lax.broadcasted_iota(jnp.int32, (members, members), 0)
    column = lax.broadcasted_iota(jnp.int32, (members, members), 1)
    eye = jnp.where(row == column, 1.0, 0.0).astype(jnp.float32)
    gram = (members - 1.0) * eye
    drive = jnp.zeros((members, 1), jnp.float32)
    for index, raw_ref in enumerate((own_ref, south_ref, north_ref)):
        raw = raw_ref[...].astype(jnp.float32)
        ybar = jnp.sum(raw, axis=0, keepdims=True) * (1.0 / members)
        pert = raw - ybar
        innov = obs_ref[index, 0:1, :] - ybar
        rloc = obs_ref[index, 1:2, :] * loc_weights(class_ref[index : index + 1, :])
        scaled = pert * rloc
        gram = gram + lax.dot_general(
            scaled,
            pert,
            (((1,), (1,)), ((), ())),
            precision=lax.Precision.HIGHEST,
            preferred_element_type=jnp.float32,
        )
        drive = drive + jnp.sum(scaled * innov, axis=1, keepdims=True)
    norm = jnp.sqrt(jnp.sum(jnp.sum(gram * gram, axis=1, keepdims=True), axis=0, keepdims=True))
    upper = gram / norm
    lower = eye
    for sweep in range(ITERS):
        factor = 1.5 * eye - 0.5 * dot(lower, upper)
        if sweep < ITERS - 1:
            upper = dot(upper, factor)
        lower = dot(factor, lower)
    wide = jnp.broadcast_to(drive, (members, members))
    wmean = dot(lower, dot(lower, wide)) / norm
    weights = (jnp.sqrt((members - 1.0) / norm) * lower + wmean).astype(jnp.bfloat16).astype(jnp.float32)
    turned = weights.T
    rest = 1.0 - jnp.sum(turned, axis=1, keepdims=True)
    rows = 8
    rest_ref[...] = jnp.broadcast_to(rest[:, :, None], (members, rows, LANES)).reshape(members * rows, LANES)
    spread = jnp.broadcast_to(turned[:, None, :], (members, rows, members)).reshape(members * rows, members)
    held = lax.broadcasted_iota(jnp.int32, (members * rows, members), 0) % rows
    for index, value in enumerate((2, 3, 4, 5, 0, 1, 6, 7)):
        mix_ref[:, index * members : (index + 1) * members] = jnp.where(held == value, spread, 0.0).astype(jnp.bfloat16)


def tile_mix(own, south, north, obs, classes):
    members = own.shape[0]
    return pl.pallas_call(
        weights_kernel,
        out_shape=[
            jax.ShapeDtypeStruct((members * 8, members * 8), jnp.bfloat16),
            jax.ShapeDtypeStruct((members * 8, LANES), jnp.float32),
        ],
        compiler_params=params(),
        cost_estimate=cost(12),
        name="weights",
    )(own, south, north, obs, classes)


def mix_kernel(mix_ref, rest_ref, inner_ref, outer_ref, out_ref):
    groups, each, part = inner_ref.shape
    members = groups * each
    width = part // 4
    inner = inner_ref[...].reshape(members, part)
    outer_part = outer_ref[...].reshape(members, part)
    pieces = [inner[:, i * width : (i + 1) * width] for i in range(4)]
    pieces += [outer_part[:, i * width : (i + 1) * width] for i in range(4)]
    stacked = jnp.concatenate(pieces, axis=0)
    rows = 8
    at = lax.broadcasted_iota(jnp.int32, (rows, members * rows), 0)
    slot = lax.broadcasted_iota(jnp.int32, (rows, members * rows), 1) // members
    source = jnp.zeros((rows, members * rows), jnp.int32)
    for index, value in enumerate((2, 3, 4, 5, 0, 1, 6, 7)):
        source = jnp.where(slot == index, value, source)
    ones = jnp.where(at == source, 1.0, 0.0).astype(jnp.bfloat16)
    mean = jnp.dot(ones, stacked, preferred_element_type=jnp.float32) * (1.0 / members)
    mixed = jnp.dot(mix_ref[...], stacked, preferred_element_type=jnp.float32)
    for index in range(width // LANES):
        lanes = slice(index * LANES, (index + 1) * LANES)
        rest = rest_ref[...].reshape(members, rows, LANES)
        made = mixed[:, lanes].reshape(members, rows, LANES) + mean[None, :, lanes] * rest
        out_ref[:, :, 0, :, lanes] = made.reshape(groups, each, rows, LANES).astype(jnp.bfloat16)


def analyse(mix, rest, inner, outer_part, levels, width):
    groups, each, _ = inner.shape
    half = pl.BlockSpec((groups, each, 4 * width), lambda i: (0, 0, i))
    return pl.pallas_call(
        mix_kernel,
        grid=(levels,),
        in_specs=[
            pl.BlockSpec(mix.shape, lambda i: (0, 0)),
            pl.BlockSpec(rest.shape, lambda i: (0, 0)),
            half,
            half,
        ],
        out_specs=pl.BlockSpec((groups, each, 1, 8, width), lambda i: (0, 0, i, 0, 0)),
        out_shape=jax.ShapeDtypeStruct((groups, each, levels, 8, width), jnp.bfloat16),
        compiler_params=params(60 * 1024 * 1024),
        cost_estimate=cost(6),
        name="analyse",
    )(mix, rest, inner, outer_part)


def to_neighbours(low, high):
    devices = lax.axis_size("space")
    up = [(i, i + 1) for i in range(devices - 1)]
    down = [(i + 1, i) for i in range(devices - 1)]
    return lax.ppermute(high, "space", up), lax.ppermute(low, "space", down)


def partner(value, bit):
    devices = lax.axis_size("member")
    return lax.ppermute(value, "member", [(i, i ^ bit) for i in range(devices)])


def gather_members(value):
    devices = lax.axis_size("member")
    here = lax.axis_index("member")
    group = devices // 2
    held = jnp.stack([value] + [partner(value, bit) for bit in range(1, group)])
    inside = here % group
    held = jnp.stack([lax.dynamic_index_in_dim(held, inside ^ i, 0, keepdims=False) for i in range(group)])
    other = partner(held, group)
    own_first = here < group
    return jnp.concatenate([jnp.where(own_first, held, other), jnp.where(own_first, other, held)])


def all_to_all(blocks):
    return lax.all_to_all(blocks, "member", split_axis=0, concat_axis=0, tiled=True)


def on_device(state, wind_east, wind_north, obs_col, obs_val, obs_rinv, obs_count, loc_class):
    members, tiles, levels, rows, width = state.shape
    slots = obs_col.shape[2]

    columns = gather_members(obs_col[0, 0])
    row = (columns // width) % rows
    inside = (row >= 2) & (row < rows - 2)
    kept = jnp.where(inside, row - 2, jnp.where(row < 2, row, row - 4))
    offset = (columns // (rows * width)) * (4 * width) + kept * width + columns % width
    place = offset // LANES + jnp.where(inside, 0, levels * 4 * width // LANES)
    lane = offset % LANES

    inner = interior(state, wind_east, wind_north)
    inner, place, lane, state, wind_east, wind_north, obs_val, obs_rinv = lax.optimization_barrier(
        (inner, place, lane, state, wind_east, wind_north, obs_val, obs_rinv)
    )
    inner_tile = all_to_all(inner)

    low, high = edge_rows(state)
    below, above = to_neighbours(low, high)
    winds = jnp.stack([wind_east[:, :, 0], wind_north[:, :, 0], wind_east[:, :, rows - 1], wind_north[:, :, rows - 1]])
    winds = jnp.swapaxes(winds, 1, 2)
    wind_below, wind_above = to_neighbours(winds[0:2], winds[2:4])
    live = jnp.arange(slots, dtype=jnp.int32) < obs_count[0, 0]
    obs = jnp.stack([obs_val[0, 0], jnp.where(live, obs_rinv[0, 0], jnp.float32(0.0))])
    obs_south, obs_north = to_neighbours(obs, obs)
    outside = outer(state, wind_east, wind_north, below, above, wind_below, wind_above)
    picked = pick(place[:, None], lane[:, None], inner, outside)

    picked, inner_tile = lax.optimization_barrier((picked, inner_tile))
    raw = all_to_all(picked)
    outside, raw = lax.optimization_barrier((outside, raw))
    outer_tile = all_to_all(outside)
    raw = raw.reshape(tiles * members, slots)
    south, north = to_neighbours(raw, raw)
    mix, rest = tile_mix(raw, south, north, jnp.stack([obs, obs_south, obs_north]), loc_class[0, 0])
    updated = analyse(mix, rest, inner_tile, outer_tile, levels, width)
    final = all_to_all(updated)
    return jnp.swapaxes(final, 0, 1)


def solution(mesh):
    return jax.shard_map(
        on_device,
        mesh=mesh,
        in_specs=(
            P("member", None, None, "space", None),
            P(None, None, "space", None),
            P(None, None, "space", None),
            P("space", "member", None),
            P("space", "member", None),
            P("space", "member", None),
            P("space", "member"),
            P("space", "member", None, None),
        ),
        out_specs=P("member", None, None, "space", None),
        check_vma=False,
    )
```

```python
import functools

import jax
import jax.numpy as jnp
from jax import lax
from jax.experimental import pallas as pl
from jax.experimental.pallas import tpu as pltpu
from jax.sharding import PartitionSpec as P

ITERS = 6
LANES = 128
VMEM_LIMIT = 48 * 1024 * 1024


def params(limit=VMEM_LIMIT):
    return pltpu.CompilerParams(vmem_limit_bytes=limit)


def cost(micros):
    return pl.CostEstimate(flops=0, bytes_accessed=int(micros * 3.6e6), transcendentals=0)


def order_rows(shape, members, rows):
    at = lax.broadcasted_iota(jnp.int32, shape, 0)
    source = lax.broadcasted_iota(jnp.int32, shape, 1)
    slot = at // members
    row = jnp.zeros(shape, jnp.int32)
    for index, value in enumerate(rows):
        row = jnp.where(slot == index, value, row)
    band = 8
    return jnp.where(source == (at % members) * band + row, 1.0, 0.0).astype(jnp.bfloat16)


def tile_rows(state_ref, tile, order):
    block = state_ref[:, tile, 0].astype(jnp.float32)
    members, rows, width = block.shape
    flat = block.reshape(members * rows, width).astype(jnp.bfloat16)
    return jnp.dot(order, flat, preferred_element_type=jnp.float32)


def edges_kernel(state_ref, low_ref, high_ref):
    members, tiles, _, rows, width = state_ref.shape
    order = order_rows((4 * members, members * rows), members, (0, 1, rows - 2, rows - 1))
    for tile in range(tiles):
        moved = tile_rows(state_ref, tile, order).astype(jnp.bfloat16)
        columns = slice(tile * width, (tile + 1) * width)
        for row in range(2):
            low_ref[0, row, :, columns] = moved[row * members : (row + 1) * members]
            high_ref[0, row, :, columns] = moved[(row + 2) * members : (row + 3) * members]


def edge_rows(state):
    members, tiles, levels, rows, width = state.shape
    shape = (levels, 2, members, tiles * width)
    block = pl.BlockSpec((1, 2, members, tiles * width), lambda i: (i, 0, 0, 0))
    return pl.pallas_call(
        edges_kernel,
        grid=(levels,),
        in_specs=[pl.BlockSpec((members, tiles, 1, rows, width), lambda i: (0, 0, i, 0, 0))],
        out_specs=[block, block],
        out_shape=[jax.ShapeDtypeStruct(shape, jnp.bfloat16)] * 2,
        compiler_params=params(),
        cost_estimate=cost(3),
        name="edges",
    )(state)


def step_rows(field, made, coef, tiles, width, rows_out, first_row):
    for row in rows_out:
        at = row - first_row
        for tile in range(tiles):
            columns = slice(LANES + tile * width, LANES + (tile + 1) * width)
            padded = slice(tile * width, LANES + (tile + 1) * width)
            west = pltpu.roll(field[at, :, padded], 1, 1)[:, LANES:]
            stay = coef[0, tile, at : at + 1, :]
            east = coef[1, tile, at : at + 1, :]
            up = coef[2, tile, at : at + 1, :]
            down = coef[3, tile, at : at + 1, :]
            made[at, :, columns] = (
                stay * field[at, :, columns]
                + east * west
                + up * field[at - 1, :, columns]
                + down * field[at + 1, :, columns]
            )
        made[at, :, 0:LANES] = made[at, :, tiles * width : tiles * width + LANES]


def set_coef(coef, slots, tile, east, north):
    up = jnp.maximum(north, 0.0)
    down = -jnp.minimum(north, 0.0)
    coef[0, tile, slots, :] = 1.0 - east - up - down
    coef[1, tile, slots, :] = east
    coef[2, tile, slots, :] = up
    coef[3, tile, slots, :] = down


def interior_kernel(state_ref, east_ref, north_ref, out_ref, field, made, coef):
    members, tiles, _, rows, width = state_ref.shape
    order = order_rows((rows * members, members * rows), members, tuple(range(rows)))
    for tile in range(tiles):
        moved = tile_rows(state_ref, tile, order)
        columns = slice(LANES + tile * width, LANES + (tile + 1) * width)
        for row in range(rows):
            field[row, :, columns] = moved[row * members : (row + 1) * members]
        set_coef(coef, slice(0, rows), tile, east_ref[tile, 0], north_ref[tile, 0])
    for row in range(rows):
        field[row, :, 0:LANES] = field[row, :, tiles * width : tiles * width + LANES]
    step_rows(field, made, coef, tiles, width, range(1, rows - 1), 0)
    step_rows(made, field, coef, tiles, width, range(2, rows - 2), 0)
    for row in range(2, rows - 2):
        for tile in range(tiles):
            columns = slice(LANES + tile * width, LANES + (tile + 1) * width)
            kept = slice((row - 2) * width, (row - 1) * width)
            out_ref[tile, :, kept] = field[row, :, columns].astype(jnp.bfloat16)


def interior(state, wind_east, wind_north):
    members, tiles, levels, rows, width = state.shape
    wind = pl.BlockSpec((tiles, 1, rows, width), lambda i: (0, i, 0, 0))
    part = (rows - 4) * width
    return pl.pallas_call(
        interior_kernel,
        grid=(levels,),
        in_specs=[pl.BlockSpec((members, tiles, 1, rows, width), lambda i: (0, 0, i, 0, 0)), wind, wind],
        out_specs=pl.BlockSpec((tiles, members, part), lambda i: (0, 0, i)),
        out_shape=jax.ShapeDtypeStruct((tiles, members, levels * part), jnp.bfloat16),
        scratch_shapes=[
            pltpu.VMEM((rows, members, LANES + tiles * width), jnp.float32),
            pltpu.VMEM((rows, members, LANES + tiles * width), jnp.float32),
            pltpu.VMEM((4, tiles, rows, width), jnp.float32),
        ],
        compiler_params=params(60 * 1024 * 1024),
        cost_estimate=cost(8),
        name="interior",
    )(state, wind_east, wind_north)


def outer_kernel(
    state_ref, east_ref, north_ref, below_ref, above_ref, wind_below_ref, wind_above_ref, out_ref, field, made, coef
):
    members, tiles, _, rows, width = state_ref.shape
    order = order_rows((rows * members, members * rows), members, tuple(range(rows)))
    for tile in range(tiles):
        moved = tile_rows(state_ref, tile, order)
        columns = slice(LANES + tile * width, LANES + (tile + 1) * width)
        for row in range(rows):
            field[row + 2, :, columns] = moved[row * members : (row + 1) * members]
        set_coef(coef, slice(2, rows + 2), tile, east_ref[tile, 0], north_ref[tile, 0])
        for slot, wind_ref in ((1, wind_below_ref), (rows + 2, wind_above_ref)):
            set_coef(
                coef,
                slice(slot, slot + 1),
                tile,
                wind_ref[0, 0, tile : tile + 1, :],
                wind_ref[1, 0, tile : tile + 1, :],
            )
    for row in range(2):
        field[row, :, LANES:] = below_ref[0, row].astype(jnp.float32)
        field[rows + 2 + row, :, LANES:] = above_ref[0, row].astype(jnp.float32)
    for slot in range(rows + 4):
        field[slot, :, 0:LANES] = field[slot, :, tiles * width : tiles * width + LANES]
    step_rows(field, made, coef, tiles, width, (-1, 0, 1, 2, rows - 3, rows - 2, rows - 1, rows), -2)
    step_rows(made, field, coef, tiles, width, (0, 1, rows - 2, rows - 1), -2)
    for index, row in enumerate((0, 1, rows - 2, rows - 1)):
        for tile in range(tiles):
            columns = slice(LANES + tile * width, LANES + (tile + 1) * width)
            kept = slice(index * width, (index + 1) * width)
            out_ref[tile, :, kept] = field[row + 2, :, columns].astype(jnp.bfloat16)


def outer(state, wind_east, wind_north, below, above, wind_below, wind_above):
    members, tiles, levels, rows, width = state.shape
    wind = pl.BlockSpec((tiles, 1, rows, width), lambda i: (0, i, 0, 0))
    edge = pl.BlockSpec((1, 2, members, tiles * width), lambda i: (i, 0, 0, 0))
    wind_edge = pl.BlockSpec((2, 1, tiles, width), lambda i: (0, i, 0, 0))
    part = 4 * width
    return pl.pallas_call(
        outer_kernel,
        grid=(levels,),
        in_specs=[
            pl.BlockSpec((members, tiles, 1, rows, width), lambda i: (0, 0, i, 0, 0)),
            wind,
            wind,
            edge,
            edge,
            wind_edge,
            wind_edge,
        ],
        out_specs=pl.BlockSpec((tiles, members, part), lambda i: (0, 0, i)),
        out_shape=jax.ShapeDtypeStruct((tiles, members, levels * part), jnp.bfloat16),
        scratch_shapes=[
            pltpu.VMEM((rows + 4, members, LANES + tiles * width), jnp.float32),
            pltpu.VMEM((rows + 4, members, LANES + tiles * width), jnp.float32),
            pltpu.VMEM((4, tiles, rows + 4, width), jnp.float32),
        ],
        compiler_params=params(60 * 1024 * 1024),
        cost_estimate=cost(9),
        name="outer",
    )(state, wind_east, wind_north, below, above, wind_below, wind_above)


def pick_kernel(steps, place_ref, lane_ref, part_ref, *refs):
    before_ref, raw_ref, total = refs if len(refs) == 3 else (None, *refs)
    groups, each, length = part_ref.shape
    members, slots = raw_ref.shape
    step = pl.program_id(0)
    at_lane = lax.broadcasted_iota(jnp.int32, (LANES, slots), 0)

    @pl.when(step == 0)
    def _():
        if before_ref is None:
            total[...] = jnp.zeros(total.shape, jnp.float32)
        else:
            total[...] = before_ref[...].astype(jnp.float32)

    here = place_ref[...] - step * (length // LANES)
    pieces = []
    for piece in range(length // LANES):
        wanted = jnp.where(here == piece, lane_ref[...], -1)
        pieces.append(jnp.where(at_lane == wanted, 1.0, 0.0).astype(jnp.bfloat16))
    flat = part_ref[...].reshape(members, length)
    total[...] += jnp.dot(flat, jnp.concatenate(pieces, axis=0), preferred_element_type=jnp.float32)

    @pl.when(step == steps - 1)
    def _():
        raw_ref[...] = total[...].astype(jnp.bfloat16)


def pick(place, lane, part, before=None):
    groups, each, length = part.shape
    slots = place.shape[1]
    members = groups * each
    steps = 8
    row = pl.BlockSpec((1, slots), lambda i: (0, 0))
    whole = pl.BlockSpec((members, slots), lambda i: (0, 0))
    return pl.pallas_call(
        functools.partial(pick_kernel, steps),
        grid=(steps,),
        in_specs=[row, row, pl.BlockSpec((groups, each, length // steps), lambda i: (0, 0, i))]
        + ([] if before is None else [whole]),
        out_specs=whole,
        scratch_shapes=[pltpu.VMEM((members, slots), jnp.float32)],
        out_shape=jax.ShapeDtypeStruct((members, slots), jnp.bfloat16),
        compiler_params=params(59 * 1024 * 1024),
        cost_estimate=cost(4),
        name="pick",
    )(place, lane, part, *([] if before is None else [before]))


def loc_weights(classes):
    table = (1.0, 0.55, 0.25, 0.08)
    total = jnp.zeros(classes.shape, jnp.float32)
    for index, value in enumerate(table):
        total = total + jnp.where(classes == index, jnp.float32(value), jnp.float32(0.0))
    return total


def halves_of(value):
    high = value.astype(jnp.bfloat16)
    return high, (value - high.astype(jnp.float32)).astype(jnp.bfloat16)


def product(left, right, turned=False):
    over = (((1,), (1 if turned else 0,)), ((), ()))
    dot = functools.partial(lax.dot_general, dimension_numbers=over, preferred_element_type=jnp.float32)
    (a, b), (c, d) = halves_of(left), halves_of(right)
    return dot(a, c) + (dot(a, d) + dot(b, c))


def gram_of(raw, value, rinv, classes):
    ybar = jnp.sum(raw, axis=0, keepdims=True) * (1.0 / raw.shape[0])
    pert = raw - ybar
    innov = value - ybar
    scaled = pert * (rinv * loc_weights(classes))
    return product(scaled, pert, turned=True), jnp.sum(scaled * innov, axis=1, keepdims=True)


def own_kernel(raw_ref, obs_ref, class_ref, gram_ref, drive_ref):
    gram, drive = gram_of(raw_ref[...].astype(jnp.float32), obs_ref[0:1, :], obs_ref[1:2, :], class_ref[0:1, :])
    gram_ref[...] = gram
    drive_ref[...] = jnp.broadcast_to(drive, gram.shape)


def own_gram(raw, obs, classes):
    members = raw.shape[0]
    return pl.pallas_call(
        own_kernel,
        out_shape=[jax.ShapeDtypeStruct((members, members), jnp.float32)] * 2,
        compiler_params=params(),
        cost_estimate=cost(2),
        name="own",
    )(raw, obs, classes)


ROWS_INNER = (2, 3, 4, 5)
ROWS_OUTER = (0, 1, 6, 7)
ROWS = 8
PAIR = 8


def is_inner(slot):
    return (slot >= 2) & (slot <= 5)


def set_weights(gram, drive, mix_refs, rest_refs):
    members = gram.shape[0]
    row = lax.broadcasted_iota(jnp.int32, (members, members), 0)
    column = lax.broadcasted_iota(jnp.int32, (members, members), 1)
    eye = jnp.where(row == column, 1.0, 0.0).astype(jnp.float32)
    gram = gram + (members - 1.0) * eye
    norm = jnp.sqrt(jnp.sum(jnp.sum(gram * gram, axis=1, keepdims=True), axis=0, keepdims=True))
    upper = gram / norm
    lower = eye
    for sweep in range(ITERS):
        factor = 1.5 * eye - 0.5 * (upper if sweep == 0 else product(lower, upper))
        if sweep < ITERS - 1:
            upper = product(upper, factor)
        lower = factor if sweep == 0 else product(factor, lower)
    wmean = product(lower, product(lower, drive)) / norm
    weights = (jnp.sqrt((members - 1.0) / norm) * lower + wmean).astype(jnp.bfloat16).astype(jnp.float32)
    turned = weights.T.astype(jnp.bfloat16)
    shape = (members * ROWS // 2, members)
    at = lax.broadcasted_iota(jnp.int32, shape, 0)
    slot = at % ROWS
    pair = at // ROWS
    low = (pair // PAIR) * (2 * PAIR) + pair % PAIR
    member = lax.broadcasted_iota(jnp.int32, shape, 1)

    def spread(which):
        chosen = jnp.where(member == which, 1.0, 0.0).astype(jnp.bfloat16)
        return jnp.dot(chosen, turned, preferred_element_type=jnp.float32)

    first, second = spread(low), spread(low + PAIR)
    for index, value in enumerate((first, second)):
        rest = 1.0 - jnp.sum(value, axis=1, keepdims=True)
        rest_refs[index] = jnp.broadcast_to(rest, shape).reshape(members // 2, ROWS, members)
    for index, rows in enumerate((ROWS_INNER, ROWS_OUTER)):
        home = is_inner(slot) if rows == ROWS_INNER else ~is_inner(slot)
        row = jnp.where(home, slot, (slot + 4) % ROWS)
        value = jnp.where(home, first, second)
        for place, wanted in enumerate(rows):
            columns = slice(place * members, (place + 1) * members)
            mix_refs[index, :, columns] = jnp.where(row == wanted, value, 0.0).astype(jnp.bfloat16)


def analyse_kernel(gram_ref, drive_ref, south_ref, north_ref, obs_ref, class_ref, inner_ref, outer_ref, out_ref, mix, rest):
    @pl.when(pl.program_id(0) == 0)
    def _():
        gram, drive = gram_ref[...], drive_ref[...]
        for index, raw_ref in ((1, south_ref), (2, north_ref)):
            more, push = gram_of(
                raw_ref[...].astype(jnp.float32),
                obs_ref[2 * index : 2 * index + 1, :],
                obs_ref[2 * index + 1 : 2 * index + 2, :],
                class_ref[index : index + 1, :],
            )
            gram, drive = gram + more, drive + push
        set_weights(gram, drive, mix, rest)

    groups, each, part = inner_ref.shape
    members = groups * each
    width = part // 4
    at = lax.broadcasted_iota(jnp.int32, (ROWS, members * 4), 0)
    slot = lax.broadcasted_iota(jnp.int32, (ROWS, members * 4), 1) // members
    mean = jnp.zeros((ROWS, width), jnp.float32)
    mixed = []
    for index, (part_ref, rows) in enumerate(((inner_ref, ROWS_INNER), (outer_ref, ROWS_OUTER))):
        flat = part_ref[...].reshape(members, part)
        stacked = jnp.concatenate([flat[:, i * width : (i + 1) * width] for i in range(4)], axis=0)
        source = jnp.zeros(at.shape, jnp.int32)
        for place, value in enumerate(rows):
            source = jnp.where(slot == place, value, source)
        ones = jnp.where(at == source, 1.0, 0.0).astype(jnp.bfloat16)
        mean = mean + jnp.dot(ones, stacked, preferred_element_type=jnp.float32)
        mixed.append(jnp.dot(mix[index], stacked, preferred_element_type=jnp.float32))
    mean = mean * (1.0 / members)
    shape = (members // 2, ROWS, LANES)
    home = is_inner(lax.broadcasted_iota(jnp.int32, shape, 1))
    for index in range(width // LANES):
        lanes = slice(index * LANES, (index + 1) * LANES)
        inner, outside = (value[:, lanes].reshape(shape) for value in mixed)
        low = jnp.where(home, inner, outside) + mean[None, :, lanes] * rest[0]
        high = pltpu.roll(jnp.where(home, outside, inner), 4, 1) + mean[None, :, lanes] * rest[1]
        half = (groups, PAIR, ROWS, LANES)
        out_ref[:, 0:PAIR, 0, :, lanes] = low.reshape(half).astype(jnp.bfloat16)
        out_ref[:, PAIR : 2 * PAIR, 0, :, lanes] = high.reshape(half).astype(jnp.bfloat16)


def analyse(gram, drive, south, north, obs, classes, inner, outer_part, levels, width):
    groups, each, _ = inner.shape
    members = groups * each
    half = pl.BlockSpec((groups, each, 4 * width), lambda i: (0, 0, i))
    small = [gram, drive, south, north, obs, classes]
    return pl.pallas_call(
        analyse_kernel,
        grid=(levels,),
        in_specs=[pl.BlockSpec(a.shape, lambda i: (0, 0)) for a in small] + [half, half],
        out_specs=pl.BlockSpec((groups, each, 1, 8, width), lambda i: (0, 0, i, 0, 0)),
        out_shape=jax.ShapeDtypeStruct((groups, each, levels, 8, width), jnp.bfloat16),
        scratch_shapes=[
            pltpu.VMEM((2, members * ROWS // 2, members * 4), jnp.bfloat16),
            pltpu.VMEM((2, members // 2, ROWS, members), jnp.float32),
        ],
        compiler_params=params(59 * 1024 * 1024),
        cost_estimate=cost(12),
        name="analyse",
    )(*small, inner, outer_part)


def to_neighbours(low, high):
    devices = lax.axis_size("space")
    up = [(i, i + 1) for i in range(devices - 1)]
    down = [(i + 1, i) for i in range(devices - 1)]
    return lax.ppermute(high, "space", up), lax.ppermute(low, "space", down)


def all_to_all(blocks):
    return lax.all_to_all(blocks, "member", split_axis=0, concat_axis=0, tiled=True)


def on_device(state, wind_east, wind_north, obs_col, obs_val, obs_rinv, obs_count, loc_class):
    members, tiles, levels, rows, width = state.shape
    slots = obs_col.shape[2]

    inner = interior(state, wind_east, wind_north)
    inner, state, wind_east, wind_north, obs_val, obs_rinv = lax.optimization_barrier(
        (inner, state, wind_east, wind_north, obs_val, obs_rinv)
    )
    inner_tile = all_to_all(inner)

    low, high = edge_rows(state)
    below, above = to_neighbours(low, high)
    winds = jnp.stack([wind_east[:, :, 0], wind_north[:, :, 0], wind_east[:, :, rows - 1], wind_north[:, :, rows - 1]])
    winds = jnp.swapaxes(winds, 1, 2)
    wind_below, wind_above = to_neighbours(winds[0:2], winds[2:4])
    live = jnp.arange(slots, dtype=jnp.int32) < obs_count[0, 0]
    obs = jnp.stack([obs_val[0, 0], jnp.where(live, obs_rinv[0, 0], jnp.float32(0.0))])
    obs_south, obs_north = to_neighbours(obs, obs)
    outside = outer(state, wind_east, wind_north, below, above, wind_below, wind_above)

    columns = obs_col[0]
    row = (columns // width) % rows
    inside = (row >= 2) & (row < rows - 2)
    kept = jnp.where(inside, row - 2, jnp.where(row < 2, row, row - 4))
    offset = (columns // (rows * width)) * (4 * width) + kept * width + columns % width
    place, lane = offset // LANES, offset % LANES

    outside, obs_south, obs_north, inner_tile = lax.optimization_barrier((outside, obs_south, obs_north, inner_tile))
    outer_tile = all_to_all(outside)
    raw = pick(jnp.where(inside, place, -1), lane, inner_tile)
    raw = pick(jnp.where(inside, -1, place), lane, outer_tile, raw)
    south, north = to_neighbours(raw, raw)
    gram, drive = own_gram(raw, obs, loc_class[0, 0])
    all_obs = jnp.concatenate([obs, obs_south, obs_north])
    updated = analyse(gram, drive, south, north, all_obs, loc_class[0, 0], inner_tile, outer_tile, levels, width)
    final = all_to_all(updated)
    return jnp.swapaxes(final, 0, 1)


def solution(mesh):
    return jax.shard_map(
        on_device,
        mesh=mesh,
        in_specs=(
            P("member", None, None, "space", None),
            P(None, None, "space", None),
            P(None, None, "space", None),
            P("space", "member", None),
            P("space", "member", None),
            P("space", "member", None),
            P("space", "member"),
            P("space", "member", None, None),
        ),
        out_specs=P("member", None, None, "space", None),
        check_vma=False,
    )
```

```python
import functools

import jax
import jax.numpy as jnp
from jax import lax
from jax.experimental import pallas as pl
from jax.experimental.pallas import tpu as pltpu
from jax.sharding import PartitionSpec as P

ITERS = 6
LANES = 128
VMEM_LIMIT = 20 * 1024 * 1024
LEAVE_ROOM = 20 * 1024 * 1024


def params(limit=VMEM_LIMIT):
    return pltpu.CompilerParams(vmem_limit_bytes=limit)


def cost(micros):
    return pl.CostEstimate(flops=0, bytes_accessed=int(micros * 3.6e6), transcendentals=0)


def order_rows(shape, members, rows):
    at = lax.broadcasted_iota(jnp.int32, shape, 0)
    source = lax.broadcasted_iota(jnp.int32, shape, 1)
    slot = at // members
    row = jnp.zeros(shape, jnp.int32)
    for index, value in enumerate(rows):
        row = jnp.where(slot == index, value, row)
    band = 8
    return jnp.where(source == (at % members) * band + row, 1.0, 0.0).astype(jnp.bfloat16)


def tile_rows(state_ref, tile, order):
    block = state_ref[:, tile, 0].astype(jnp.float32)
    members, rows, width = block.shape
    flat = block.reshape(members * rows, width).astype(jnp.bfloat16)
    return jnp.dot(order, flat, preferred_element_type=jnp.float32)


def edges_kernel(state_ref, low_ref, high_ref):
    members, tiles, _, rows, width = state_ref.shape
    order = order_rows((4 * members, members * rows), members, (0, 1, rows - 2, rows - 1))
    for tile in range(tiles):
        moved = tile_rows(state_ref, tile, order).astype(jnp.bfloat16)
        columns = slice(tile * width, (tile + 1) * width)
        for row in range(2):
            low_ref[0, row, :, columns] = moved[row * members : (row + 1) * members]
            high_ref[0, row, :, columns] = moved[(row + 2) * members : (row + 3) * members]


def edge_rows(state):
    members, tiles, levels, rows, width = state.shape
    shape = (levels, 2, members, tiles * width)
    block = pl.BlockSpec((1, 2, members, tiles * width), lambda i: (i, 0, 0, 0))
    return pl.pallas_call(
        edges_kernel,
        grid=(levels,),
        in_specs=[pl.BlockSpec((members, tiles, 1, rows, width), lambda i: (0, 0, i, 0, 0))],
        out_specs=[block, block],
        out_shape=[jax.ShapeDtypeStruct(shape, jnp.bfloat16)] * 2,
        compiler_params=params(),
        cost_estimate=cost(3),
        name="edges",
    )(state)


def step_rows(field, made, coef, tiles, width, rows_out, first_row):
    for row in rows_out:
        at = row - first_row
        for tile in range(tiles):
            columns = slice(LANES + tile * width, LANES + (tile + 1) * width)
            padded = slice(tile * width, LANES + (tile + 1) * width)
            west = pltpu.roll(field[at, :, padded], 1, 1)[:, LANES:]
            stay = coef[0, tile, at : at + 1, :]
            east = coef[1, tile, at : at + 1, :]
            up = coef[2, tile, at : at + 1, :]
            down = coef[3, tile, at : at + 1, :]
            made[at, :, columns] = (
                stay * field[at, :, columns]
                + east * west
                + up * field[at - 1, :, columns]
                + down * field[at + 1, :, columns]
            )
        made[at, :, 0:LANES] = made[at, :, tiles * width : tiles * width + LANES]


def set_coef(coef, slots, tile, east, north):
    up = jnp.maximum(north, 0.0)
    down = -jnp.minimum(north, 0.0)
    coef[0, tile, slots, :] = 1.0 - east - up - down
    coef[1, tile, slots, :] = east
    coef[2, tile, slots, :] = up
    coef[3, tile, slots, :] = down


def interior_kernel(state_ref, east_ref, north_ref, out_ref, field, made, coef):
    members, tiles, _, rows, width = state_ref.shape
    order = order_rows((rows * members, members * rows), members, tuple(range(rows)))
    for tile in range(tiles):
        moved = tile_rows(state_ref, tile, order)
        columns = slice(LANES + tile * width, LANES + (tile + 1) * width)
        for row in range(rows):
            field[row, :, columns] = moved[row * members : (row + 1) * members]
        set_coef(coef, slice(0, rows), tile, east_ref[tile, 0], north_ref[tile, 0])
    for row in range(rows):
        field[row, :, 0:LANES] = field[row, :, tiles * width : tiles * width + LANES]
    step_rows(field, made, coef, tiles, width, range(1, rows - 1), 0)
    step_rows(made, field, coef, tiles, width, range(2, rows - 2), 0)
    for row in range(2, rows - 2):
        for tile in range(tiles):
            columns = slice(LANES + tile * width, LANES + (tile + 1) * width)
            kept = slice((row - 2) * width, (row - 1) * width)
            out_ref[tile, :, kept] = field[row, :, columns].astype(jnp.bfloat16)


def interior(state, wind_east, wind_north):
    members, tiles, levels, rows, width = state.shape
    wind = pl.BlockSpec((tiles, 1, rows, width), lambda i: (0, i, 0, 0))
    part = (rows - 4) * width
    return pl.pallas_call(
        interior_kernel,
        grid=(levels,),
        in_specs=[pl.BlockSpec((members, tiles, 1, rows, width), lambda i: (0, 0, i, 0, 0)), wind, wind],
        out_specs=pl.BlockSpec((tiles, members, part), lambda i: (0, 0, i)),
        out_shape=jax.ShapeDtypeStruct((tiles, members, levels * part), jnp.bfloat16),
        scratch_shapes=[
            pltpu.VMEM((rows, members, LANES + tiles * width), jnp.float32),
            pltpu.VMEM((rows, members, LANES + tiles * width), jnp.float32),
            pltpu.VMEM((4, tiles, rows, width), jnp.float32),
        ],
        compiler_params=params(60 * 1024 * 1024),
        cost_estimate=cost(8),
        name="interior",
    )(state, wind_east, wind_north)


def outer_kernel(
    state_ref, east_ref, north_ref, below_ref, above_ref, wind_below_ref, wind_above_ref, out_ref, field, made, coef
):
    members, tiles, _, rows, width = state_ref.shape
    order = order_rows((rows * members, members * rows), members, tuple(range(rows)))
    for tile in range(tiles):
        moved = tile_rows(state_ref, tile, order)
        columns = slice(LANES + tile * width, LANES + (tile + 1) * width)
        for row in range(rows):
            field[row + 2, :, columns] = moved[row * members : (row + 1) * members]
        set_coef(coef, slice(2, rows + 2), tile, east_ref[tile, 0], north_ref[tile, 0])
        for slot, wind_ref in ((1, wind_below_ref), (rows + 2, wind_above_ref)):
            set_coef(
                coef,
                slice(slot, slot + 1),
                tile,
                wind_ref[0, 0, tile : tile + 1, :],
                wind_ref[1, 0, tile : tile + 1, :],
            )
    for row in range(2):
        field[row, :, LANES:] = below_ref[0, row].astype(jnp.float32)
        field[rows + 2 + row, :, LANES:] = above_ref[0, row].astype(jnp.float32)
    for slot in range(rows + 4):
        field[slot, :, 0:LANES] = field[slot, :, tiles * width : tiles * width + LANES]
    step_rows(field, made, coef, tiles, width, (-1, 0, 1, 2, rows - 3, rows - 2, rows - 1, rows), -2)
    step_rows(made, field, coef, tiles, width, (0, 1, rows - 2, rows - 1), -2)
    for index, row in enumerate((0, 1, rows - 2, rows - 1)):
        for tile in range(tiles):
            columns = slice(LANES + tile * width, LANES + (tile + 1) * width)
            kept = slice(index * width, (index + 1) * width)
            out_ref[tile, :, kept] = field[row + 2, :, columns].astype(jnp.bfloat16)


def outer(state, wind_east, wind_north, below, above, wind_below, wind_above):
    members, tiles, levels, rows, width = state.shape
    wind = pl.BlockSpec((tiles, 1, rows, width), lambda i: (0, i, 0, 0))
    edge = pl.BlockSpec((1, 2, members, tiles * width), lambda i: (i, 0, 0, 0))
    wind_edge = pl.BlockSpec((2, 1, tiles, width), lambda i: (0, i, 0, 0))
    part = 4 * width
    return pl.pallas_call(
        outer_kernel,
        grid=(levels,),
        in_specs=[
            pl.BlockSpec((members, tiles, 1, rows, width), lambda i: (0, 0, i, 0, 0)),
            wind,
            wind,
            edge,
            edge,
            wind_edge,
            wind_edge,
        ],
        out_specs=pl.BlockSpec((tiles, members, part), lambda i: (0, 0, i)),
        out_shape=jax.ShapeDtypeStruct((tiles, members, levels * part), jnp.bfloat16),
        scratch_shapes=[
            pltpu.VMEM((rows + 4, members, LANES + tiles * width), jnp.float32),
            pltpu.VMEM((rows + 4, members, LANES + tiles * width), jnp.float32),
            pltpu.VMEM((4, tiles, rows + 4, width), jnp.float32),
        ],
        compiler_params=params(),
        cost_estimate=cost(9),
        name="outer",
    )(state, wind_east, wind_north, below, above, wind_below, wind_above)


def pick_kernel(span, place_ref, lane_ref, part_ref, *refs):
    before_ref, raw_ref = refs if len(refs) == 2 else (None, *refs)
    groups, each, length = part_ref.shape
    slots = raw_ref.shape[1]
    at_lane = lax.broadcasted_iota(jnp.int32, (span, slots), 0)
    chosen = jnp.where(at_lane == lane_ref[...], 1.0, 0.0).astype(jnp.bfloat16)
    place = jnp.broadcast_to(place_ref[...], (each, slots))
    together = LANES // each
    for group in range(groups):
        members = slice(group * each, (group + 1) * each)
        total = jnp.zeros((each, slots), jnp.float32) if before_ref is None else before_ref[members].astype(jnp.float32)
        for first in range(0, length // span, together):
            pieces = [part_ref[group, :, (first + i) * span : (first + i + 1) * span] for i in range(together)]
            found = jnp.dot(jnp.concatenate(pieces, axis=0), chosen, preferred_element_type=jnp.float32)
            for i in range(together):
                total = jnp.where(place == first + i, found[i * each : (i + 1) * each], total)
        raw_ref[members] = total.astype(jnp.bfloat16)


def pick(place, lane, part, span, before=None):
    groups, each, length = part.shape
    slots = place.shape[1]
    steps = 2
    row = pl.BlockSpec((1, slots), lambda i: (0, 0))
    some = pl.BlockSpec((groups // steps * each, slots), lambda i: (i, 0))
    return pl.pallas_call(
        functools.partial(pick_kernel, span),
        grid=(steps,),
        in_specs=[row, row, pl.BlockSpec((groups // steps, each, length), lambda i: (i, 0, 0))]
        + ([] if before is None else [some]),
        out_specs=some,
        out_shape=jax.ShapeDtypeStruct((groups * each, slots), jnp.bfloat16),
        compiler_params=params(LEAVE_ROOM),
        cost_estimate=cost(4),
        name="pick",
    )(place, lane, part, *([] if before is None else [before]))


def loc_weights(classes):
    table = (1.0, 0.55, 0.25, 0.08)
    total = jnp.zeros(classes.shape, jnp.float32)
    for index, value in enumerate(table):
        total = total + jnp.where(classes == index, jnp.float32(value), jnp.float32(0.0))
    return total


def halves_of(value):
    high = value.astype(jnp.bfloat16)
    return high, (value - high.astype(jnp.float32)).astype(jnp.bfloat16)


def product(left, right, turned=False):
    over = (((1,), (1 if turned else 0,)), ((), ()))
    dot = functools.partial(lax.dot_general, dimension_numbers=over, preferred_element_type=jnp.float32)
    (a, b), (c, d) = halves_of(left), halves_of(right)
    return dot(a, c) + (dot(a, d) + dot(b, c))


def gram_of(raw, value, rinv, classes):
    ybar = jnp.sum(raw, axis=0, keepdims=True) * (1.0 / raw.shape[0])
    pert = raw - ybar
    innov = value - ybar
    scaled = pert * (rinv * loc_weights(classes))
    return product(scaled, pert, turned=True), jnp.sum(scaled * innov, axis=1, keepdims=True)


ROWS_INNER = (2, 3, 4, 5)
ROWS_OUTER = (0, 1, 6, 7)
ROWS = 8
PAIR = 8


def is_inner(slot):
    return (slot >= 2) & (slot <= 5)


def set_weights(gram, drive, mix_refs, rest_refs):
    members = gram.shape[0]
    row = lax.broadcasted_iota(jnp.int32, (members, members), 0)
    column = lax.broadcasted_iota(jnp.int32, (members, members), 1)
    eye = jnp.where(row == column, 1.0, 0.0).astype(jnp.float32)
    gram = gram + (members - 1.0) * eye
    norm = jnp.sqrt(jnp.sum(jnp.sum(gram * gram, axis=1, keepdims=True), axis=0, keepdims=True))
    upper = gram / norm
    lower = eye
    for sweep in range(ITERS):
        factor = 1.5 * eye - 0.5 * (upper if sweep == 0 else product(lower, upper))
        if sweep < ITERS - 1:
            upper = product(upper, factor)
        lower = factor if sweep == 0 else product(factor, lower)
    wmean = product(lower, product(lower, drive)) / norm
    weights = (jnp.sqrt((members - 1.0) / norm) * lower + wmean).astype(jnp.bfloat16).astype(jnp.float32)
    turned = weights.T.astype(jnp.bfloat16)
    shape = (members * ROWS // 2, members)
    at = lax.broadcasted_iota(jnp.int32, shape, 0)
    slot = at % ROWS
    pair = at // ROWS
    low = (pair // PAIR) * (2 * PAIR) + pair % PAIR
    member = lax.broadcasted_iota(jnp.int32, shape, 1)

    def spread(which):
        chosen = jnp.where(member == which, 1.0, 0.0).astype(jnp.bfloat16)
        return jnp.dot(chosen, turned, preferred_element_type=jnp.float32)

    first, second = spread(low), spread(low + PAIR)
    for index, value in enumerate((first, second)):
        rest = 1.0 - jnp.sum(value, axis=1, keepdims=True)
        rest_refs[index] = jnp.broadcast_to(rest, shape).reshape(members // 2, ROWS, members)
    for index, rows in enumerate((ROWS_INNER, ROWS_OUTER)):
        home = is_inner(slot) if rows == ROWS_INNER else ~is_inner(slot)
        row = jnp.where(home, slot, (slot + 4) % ROWS)
        value = jnp.where(home, first, second)
        for place, wanted in enumerate(rows):
            columns = slice(place * members, (place + 1) * members)
            mix_refs[index, :, columns] = jnp.where(row == wanted, value, 0.0).astype(jnp.bfloat16)


def analyse_kernel(own_ref, south_ref, north_ref, obs_ref, class_ref, inner_ref, outer_ref, out_ref, mix, rest):
    @pl.when(pl.program_id(0) == 0)
    def _():
        gram = drive = 0.0
        for index, raw_ref in enumerate((own_ref, south_ref, north_ref)):
            more, push = gram_of(
                raw_ref[...].astype(jnp.float32),
                obs_ref[2 * index : 2 * index + 1, :],
                obs_ref[2 * index + 1 : 2 * index + 2, :],
                class_ref[index : index + 1, :],
            )
            gram, drive = gram + more, drive + push
        set_weights(gram, jnp.broadcast_to(drive, gram.shape), mix, rest)

    groups, each, part = inner_ref.shape
    members = groups * each
    width = part // 4
    at = lax.broadcasted_iota(jnp.int32, (ROWS, members * 4), 0)
    slot = lax.broadcasted_iota(jnp.int32, (ROWS, members * 4), 1) // members
    mean = jnp.zeros((ROWS, width), jnp.float32)
    mixed = []
    for index, (part_ref, rows) in enumerate(((inner_ref, ROWS_INNER), (outer_ref, ROWS_OUTER))):
        flat = part_ref[...].reshape(members, part)
        stacked = jnp.concatenate([flat[:, i * width : (i + 1) * width] for i in range(4)], axis=0)
        source = jnp.zeros(at.shape, jnp.int32)
        for place, value in enumerate(rows):
            source = jnp.where(slot == place, value, source)
        ones = jnp.where(at == source, 1.0, 0.0).astype(jnp.bfloat16)
        mean = mean + jnp.dot(ones, stacked, preferred_element_type=jnp.float32)
        mixed.append(jnp.dot(mix[index], stacked, preferred_element_type=jnp.float32))
    mean = mean * (1.0 / members)
    shape = (members // 2, ROWS, LANES)
    home = is_inner(lax.broadcasted_iota(jnp.int32, shape, 1))
    for index in range(width // LANES):
        lanes = slice(index * LANES, (index + 1) * LANES)
        inner, outside = (value[:, lanes].reshape(shape) for value in mixed)
        low = jnp.where(home, inner, outside) + mean[None, :, lanes] * rest[0]
        high = pltpu.roll(jnp.where(home, outside, inner), 4, 1) + mean[None, :, lanes] * rest[1]
        half = (groups, PAIR, ROWS, LANES)
        out_ref[:, 0:PAIR, 0, :, lanes] = low.reshape(half).astype(jnp.bfloat16)
        out_ref[:, PAIR : 2 * PAIR, 0, :, lanes] = high.reshape(half).astype(jnp.bfloat16)


def analyse(raw, south, north, obs, classes, inner, outer_part, levels, width):
    groups, each, _ = inner.shape
    members = groups * each
    half = pl.BlockSpec((groups, each, 4 * width), lambda i: (0, 0, i))
    small = [raw, south, north, obs, classes]
    return pl.pallas_call(
        analyse_kernel,
        grid=(levels,),
        in_specs=[pl.BlockSpec(a.shape, lambda i: (0, 0)) for a in small] + [half, half],
        out_specs=pl.BlockSpec((groups, each, 1, 8, width), lambda i: (0, 0, i, 0, 0)),
        out_shape=jax.ShapeDtypeStruct((groups, each, levels, 8, width), jnp.bfloat16),
        scratch_shapes=[
            pltpu.VMEM((2, members * ROWS // 2, members * 4), jnp.bfloat16),
            pltpu.VMEM((2, members // 2, ROWS, members), jnp.float32),
        ],
        compiler_params=params(LEAVE_ROOM),
        cost_estimate=cost(12),
        name="analyse",
    )(*small, inner, outer_part)


def to_neighbours(low, high):
    devices = lax.axis_size("space")
    up = [(i, i + 1) for i in range(devices - 1)]
    down = [(i + 1, i) for i in range(devices - 1)]
    return lax.ppermute(high, "space", up), lax.ppermute(low, "space", down)


def all_to_all(blocks):
    return lax.all_to_all(blocks, "member", split_axis=0, concat_axis=0, tiled=True)


def on_device(state, wind_east, wind_north, obs_col, obs_val, obs_rinv, obs_count, loc_class):
    members, tiles, levels, rows, width = state.shape
    slots = obs_col.shape[2]

    inner = interior(state, wind_east, wind_north)
    inner, state, wind_east, wind_north, obs_val, obs_rinv = lax.optimization_barrier(
        (inner, state, wind_east, wind_north, obs_val, obs_rinv)
    )
    inner_tile = all_to_all(inner)

    low, high = edge_rows(state)
    below, above = to_neighbours(low, high)
    winds = jnp.stack([wind_east[:, :, 0], wind_north[:, :, 0], wind_east[:, :, rows - 1], wind_north[:, :, rows - 1]])
    winds = jnp.swapaxes(winds, 1, 2)
    wind_below, wind_above = to_neighbours(winds[0:2], winds[2:4])
    live = jnp.arange(slots, dtype=jnp.int32) < obs_count[0, 0]
    obs = jnp.stack([obs_val[0, 0], jnp.where(live, obs_rinv[0, 0], jnp.float32(0.0))])
    obs_south, obs_north = to_neighbours(obs, obs)
    outside = outer(state, wind_east, wind_north, below, above, wind_below, wind_above)

    columns = obs_col[0]
    row = (columns // width) % rows
    inside = (row >= 2) & (row < rows - 2)
    kept = jnp.where(inside, row - 2, jnp.where(row < 2, row, row - 4))
    offset = (columns // (rows * width)) * (4 * width) + kept * width + columns % width
    span = 2 * LANES
    place, lane = offset // span, offset % span

    all_obs = jnp.concatenate([obs, obs_south, obs_north])
    outside, all_obs, inner_tile = lax.optimization_barrier((outside, all_obs, inner_tile))
    outer_tile = all_to_all(outside)
    raw = pick(jnp.where(inside, place, -1), lane, inner_tile, span)
    raw = pick(jnp.where(inside, -1, place), lane, outer_tile, span, raw)
    south, north = to_neighbours(raw, raw)
    updated = analyse(raw, south, north, all_obs, loc_class[0, 0], inner_tile, outer_tile, levels, width)
    final = all_to_all(updated)
    return jnp.swapaxes(final, 0, 1)


def solution(mesh):
    return jax.shard_map(
        on_device,
        mesh=mesh,
        in_specs=(
            P("member", None, None, "space", None),
            P(None, None, "space", None),
            P(None, None, "space", None),
            P("space", "member", None),
            P("space", "member", None),
            P("space", "member", None),
            P("space", "member"),
            P("space", "member", None, None),
        ),
        out_specs=P("member", None, None, "space", None),
        check_vma=False,
    )
```

```python
import functools

import jax
import jax.numpy as jnp
from jax import lax
from jax.experimental import pallas as pl
from jax.experimental.pallas import tpu as pltpu
from jax.sharding import PartitionSpec as P

ITERS = 6
LANES = 128
VMEM_LIMIT = 14 * 1024 * 1024
LEAVE_ROOM = 14 * 1024 * 1024


def params(limit=VMEM_LIMIT):
    return pltpu.CompilerParams(vmem_limit_bytes=limit)


def cost(micros):
    return pl.CostEstimate(flops=0, bytes_accessed=int(micros * 3.6e6), transcendentals=0)


def order_rows(shape, members, rows):
    at = lax.broadcasted_iota(jnp.int32, shape, 0)
    source = lax.broadcasted_iota(jnp.int32, shape, 1)
    slot = at // members
    row = jnp.zeros(shape, jnp.int32)
    for index, value in enumerate(rows):
        row = jnp.where(slot == index, value, row)
    band = 8
    return jnp.where(source == (at % members) * band + row, 1.0, 0.0).astype(jnp.bfloat16)


def tile_rows(state_ref, tile, order):
    block = state_ref[:, tile, 0].astype(jnp.float32)
    members, rows, width = block.shape
    flat = block.reshape(members * rows, width).astype(jnp.bfloat16)
    return jnp.dot(order, flat, preferred_element_type=jnp.float32)


def edges_kernel(state_ref, low_ref, high_ref):
    members, tiles, _, rows, width = state_ref.shape
    order = order_rows((4 * members, members * rows), members, (0, 1, rows - 2, rows - 1))
    for tile in range(tiles):
        moved = tile_rows(state_ref, tile, order).astype(jnp.bfloat16)
        columns = slice(tile * width, (tile + 1) * width)
        for row in range(2):
            low_ref[0, row, :, columns] = moved[row * members : (row + 1) * members]
            high_ref[0, row, :, columns] = moved[(row + 2) * members : (row + 3) * members]


def edge_rows(state):
    members, tiles, levels, rows, width = state.shape
    shape = (levels, 2, members, tiles * width)
    block = pl.BlockSpec((1, 2, members, tiles * width), lambda i: (i, 0, 0, 0))
    return pl.pallas_call(
        edges_kernel,
        grid=(levels,),
        in_specs=[pl.BlockSpec((members, tiles, 1, rows, width), lambda i: (0, 0, i, 0, 0))],
        out_specs=[block, block],
        out_shape=[jax.ShapeDtypeStruct(shape, jnp.bfloat16)] * 2,
        compiler_params=params(),
        cost_estimate=cost(3),
        name="edges",
    )(state)


def step_rows(field, made, coef, tiles, width, rows_out, first_row):
    for row in rows_out:
        at = row - first_row
        for tile in range(tiles):
            columns = slice(LANES + tile * width, LANES + (tile + 1) * width)
            padded = slice(tile * width, LANES + (tile + 1) * width)
            west = pltpu.roll(field[at, :, padded], 1, 1)[:, LANES:]
            stay = coef[0, tile, at : at + 1, :]
            east = coef[1, tile, at : at + 1, :]
            up = coef[2, tile, at : at + 1, :]
            down = coef[3, tile, at : at + 1, :]
            made[at, :, columns] = (
                stay * field[at, :, columns]
                + east * west
                + up * field[at - 1, :, columns]
                + down * field[at + 1, :, columns]
            )
        made[at, :, 0:LANES] = made[at, :, tiles * width : tiles * width + LANES]


def set_coef(coef, slots, tile, east, north):
    up = jnp.maximum(north, 0.0)
    down = -jnp.minimum(north, 0.0)
    coef[0, tile, slots, :] = 1.0 - east - up - down
    coef[1, tile, slots, :] = east
    coef[2, tile, slots, :] = up
    coef[3, tile, slots, :] = down


def interior_kernel(state_ref, east_ref, north_ref, out_ref, field, made, coef):
    members, tiles, _, rows, width = state_ref.shape
    order = order_rows((rows * members, members * rows), members, tuple(range(rows)))
    for tile in range(tiles):
        moved = tile_rows(state_ref, tile, order)
        columns = slice(LANES + tile * width, LANES + (tile + 1) * width)
        for row in range(rows):
            field[row, :, columns] = moved[row * members : (row + 1) * members]
        set_coef(coef, slice(0, rows), tile, east_ref[tile, 0], north_ref[tile, 0])
    for row in range(rows):
        field[row, :, 0:LANES] = field[row, :, tiles * width : tiles * width + LANES]
    step_rows(field, made, coef, tiles, width, range(1, rows - 1), 0)
    step_rows(made, field, coef, tiles, width, range(2, rows - 2), 0)
    for row in range(2, rows - 2):
        for tile in range(tiles):
            columns = slice(LANES + tile * width, LANES + (tile + 1) * width)
            kept = slice((row - 2) * width, (row - 1) * width)
            out_ref[tile, :, kept] = field[row, :, columns].astype(jnp.bfloat16)


def interior(state, wind_east, wind_north):
    members, tiles, levels, rows, width = state.shape
    wind = pl.BlockSpec((tiles, 1, rows, width), lambda i: (0, i, 0, 0))
    part = (rows - 4) * width
    return pl.pallas_call(
        interior_kernel,
        grid=(levels,),
        in_specs=[pl.BlockSpec((members, tiles, 1, rows, width), lambda i: (0, 0, i, 0, 0)), wind, wind],
        out_specs=pl.BlockSpec((tiles, members, part), lambda i: (0, 0, i)),
        out_shape=jax.ShapeDtypeStruct((tiles, members, levels * part), jnp.bfloat16),
        scratch_shapes=[
            pltpu.VMEM((rows, members, LANES + tiles * width), jnp.float32),
            pltpu.VMEM((rows, members, LANES + tiles * width), jnp.float32),
            pltpu.VMEM((4, tiles, rows, width), jnp.float32),
        ],
        compiler_params=params(60 * 1024 * 1024),
        cost_estimate=cost(8),
        name="interior",
    )(state, wind_east, wind_north)


def outer_kernel(
    state_ref, east_ref, north_ref, below_ref, above_ref, wind_below_ref, wind_above_ref, out_ref, field, made, coef
):
    members, tiles, _, rows, width = state_ref.shape
    order = order_rows((rows * members, members * rows), members, tuple(range(rows)))
    for tile in range(tiles):
        moved = tile_rows(state_ref, tile, order)
        columns = slice(LANES + tile * width, LANES + (tile + 1) * width)
        for row in range(rows):
            field[row + 2, :, columns] = moved[row * members : (row + 1) * members]
        set_coef(coef, slice(2, rows + 2), tile, east_ref[tile, 0], north_ref[tile, 0])
        for slot, wind_ref in ((1, wind_below_ref), (rows + 2, wind_above_ref)):
            set_coef(
                coef,
                slice(slot, slot + 1),
                tile,
                wind_ref[0, 0, tile : tile + 1, :],
                wind_ref[1, 0, tile : tile + 1, :],
            )
    for row in range(2):
        field[row, :, LANES:] = below_ref[0, row].astype(jnp.float32)
        field[rows + 2 + row, :, LANES:] = above_ref[0, row].astype(jnp.float32)
    for slot in range(rows + 4):
        field[slot, :, 0:LANES] = field[slot, :, tiles * width : tiles * width + LANES]
    step_rows(field, made, coef, tiles, width, (-1, 0, 1, 2, rows - 3, rows - 2, rows - 1, rows), -2)
    step_rows(made, field, coef, tiles, width, (0, 1, rows - 2, rows - 1), -2)
    for index, row in enumerate((0, 1, rows - 2, rows - 1)):
        for tile in range(tiles):
            columns = slice(LANES + tile * width, LANES + (tile + 1) * width)
            kept = slice(index * width, (index + 1) * width)
            out_ref[tile, :, kept] = field[row + 2, :, columns].astype(jnp.bfloat16)


def outer(state, wind_east, wind_north, below, above, wind_below, wind_above):
    members, tiles, levels, rows, width = state.shape
    wind = pl.BlockSpec((tiles, 1, rows, width), lambda i: (0, i, 0, 0))
    edge = pl.BlockSpec((1, 2, members, tiles * width), lambda i: (i, 0, 0, 0))
    wind_edge = pl.BlockSpec((2, 1, tiles, width), lambda i: (0, i, 0, 0))
    part = 4 * width
    return pl.pallas_call(
        outer_kernel,
        grid=(levels,),
        in_specs=[
            pl.BlockSpec((members, tiles, 1, rows, width), lambda i: (0, 0, i, 0, 0)),
            wind,
            wind,
            edge,
            edge,
            wind_edge,
            wind_edge,
        ],
        out_specs=pl.BlockSpec((tiles, members, part), lambda i: (0, 0, i)),
        out_shape=jax.ShapeDtypeStruct((tiles, members, levels * part), jnp.bfloat16),
        scratch_shapes=[
            pltpu.VMEM((rows + 4, members, LANES + tiles * width), jnp.float32),
            pltpu.VMEM((rows + 4, members, LANES + tiles * width), jnp.float32),
            pltpu.VMEM((4, tiles, rows + 4, width), jnp.float32),
        ],
        compiler_params=params(),
        cost_estimate=cost(9),
        name="outer",
    )(state, wind_east, wind_north, below, above, wind_below, wind_above)


def pick_kernel(span, place_ref, lane_ref, part_ref, *refs):
    before_ref, raw_ref = refs if len(refs) == 2 else (None, *refs)
    groups, each, length = part_ref.shape
    slots = raw_ref.shape[1]
    at_lane = lax.broadcasted_iota(jnp.int32, (span, slots), 0)
    chosen = jnp.where(at_lane == lane_ref[...], 1.0, 0.0).astype(jnp.bfloat16)
    place = jnp.broadcast_to(place_ref[...], (each, slots))
    together = LANES // each
    for group in range(groups):
        members = slice(group * each, (group + 1) * each)
        total = jnp.zeros((each, slots), jnp.float32) if before_ref is None else before_ref[members].astype(jnp.float32)
        for first in range(0, length // span, together):
            pieces = [part_ref[group, :, (first + i) * span : (first + i + 1) * span] for i in range(together)]
            found = jnp.dot(jnp.concatenate(pieces, axis=0), chosen, preferred_element_type=jnp.float32)
            for i in range(together):
                total = jnp.where(place == first + i, found[i * each : (i + 1) * each], total)
        raw_ref[members] = total.astype(jnp.bfloat16)


def pick(place, lane, part, span, before=None):
    groups, each, length = part.shape
    slots = place.shape[1]
    steps = 2
    row = pl.BlockSpec((1, slots), lambda i: (0, 0))
    some = pl.BlockSpec((groups // steps * each, slots), lambda i: (i, 0))
    return pl.pallas_call(
        functools.partial(pick_kernel, span),
        grid=(steps,),
        in_specs=[row, row, pl.BlockSpec((groups // steps, each, length), lambda i: (i, 0, 0))]
        + ([] if before is None else [some]),
        out_specs=some,
        out_shape=jax.ShapeDtypeStruct((groups * each, slots), jnp.bfloat16),
        compiler_params=params(LEAVE_ROOM),
        cost_estimate=cost(4),
        name="pick",
    )(place, lane, part, *([] if before is None else [before]))


def loc_weights(classes):
    table = (1.0, 0.55, 0.25, 0.08)
    total = jnp.zeros(classes.shape, jnp.float32)
    for index, value in enumerate(table):
        total = total + jnp.where(classes == index, jnp.float32(value), jnp.float32(0.0))
    return total


def halves_of(value):
    high = value.astype(jnp.bfloat16)
    return high, (value - high.astype(jnp.float32)).astype(jnp.bfloat16)


def product(left, right, turned=False):
    over = (((1,), (1 if turned else 0,)), ((), ()))
    dot = functools.partial(lax.dot_general, dimension_numbers=over, preferred_element_type=jnp.float32)
    (a, b), (c, d) = halves_of(left), halves_of(right)
    axis = 1 if turned else 0
    return dot(jnp.concatenate([a, a, b], axis=1), jnp.concatenate([c, d, c], axis=axis))


def gram_of(raw, value, rinv, classes):
    ybar = jnp.sum(raw, axis=0, keepdims=True) * (1.0 / raw.shape[0])
    pert = raw - ybar
    innov = value - ybar
    scaled = pert * (rinv * loc_weights(classes))
    return product(scaled, pert, turned=True), jnp.sum(scaled * innov, axis=1, keepdims=True)


ROWS_INNER = (2, 3, 4, 5)
ROWS_OUTER = (0, 1, 6, 7)
ROWS = 8
PAIR = 8


def is_inner(slot):
    return (slot >= 2) & (slot <= 5)


def set_weights(gram, drive, mix_refs, rest_refs):
    members = gram.shape[0]
    row = lax.broadcasted_iota(jnp.int32, (members, members), 0)
    column = lax.broadcasted_iota(jnp.int32, (members, members), 1)
    eye = jnp.where(row == column, 1.0, 0.0).astype(jnp.float32)
    gram = gram + (members - 1.0) * eye
    norm = jnp.sqrt(jnp.sum(jnp.sum(gram * gram, axis=1, keepdims=True), axis=0, keepdims=True))
    upper = gram / norm
    lower = eye
    for sweep in range(ITERS):
        factor = 1.5 * eye - 0.5 * (upper if sweep == 0 else product(lower, upper))
        if sweep < ITERS - 1:
            upper = product(upper, factor)
        lower = factor if sweep == 0 else product(factor, lower)
    wmean = product(lower, product(lower, drive)) / norm
    weights = (jnp.sqrt((members - 1.0) / norm) * lower + wmean).astype(jnp.bfloat16).astype(jnp.float32)
    turned = weights.T.astype(jnp.bfloat16)
    shape = (members * ROWS // 2, members)
    at = lax.broadcasted_iota(jnp.int32, shape, 0)
    slot = at % ROWS
    pair = at // ROWS
    low = (pair // PAIR) * (2 * PAIR) + pair % PAIR
    member = lax.broadcasted_iota(jnp.int32, shape, 1)

    def spread(which):
        chosen = jnp.where(member == which, 1.0, 0.0).astype(jnp.bfloat16)
        return jnp.dot(chosen, turned, preferred_element_type=jnp.float32)

    first, second = spread(low), spread(low + PAIR)
    for index, value in enumerate((first, second)):
        rest = 1.0 - jnp.sum(value, axis=1, keepdims=True)
        rest_refs[index] = jnp.broadcast_to(rest, shape).reshape(members // 2, ROWS, members)
    for index, rows in enumerate((ROWS_INNER, ROWS_OUTER)):
        home = is_inner(slot) if rows == ROWS_INNER else ~is_inner(slot)
        row = jnp.where(home, slot, (slot + 4) % ROWS)
        value = jnp.where(home, first, second)
        for place, wanted in enumerate(rows):
            columns = slice(place * members, (place + 1) * members)
            mix_refs[index, :, columns] = jnp.where(row == wanted, value, 0.0).astype(jnp.bfloat16)


def analyse_kernel(own_ref, south_ref, north_ref, obs_ref, class_ref, inner_ref, outer_ref, out_ref, mix, rest):
    @pl.when(pl.program_id(0) == 0)
    def _():
        gram = drive = 0.0
        for index, raw_ref in enumerate((own_ref, south_ref, north_ref)):
            more, push = gram_of(
                raw_ref[...].astype(jnp.float32),
                obs_ref[2 * index : 2 * index + 1, :],
                obs_ref[2 * index + 1 : 2 * index + 2, :],
                class_ref[index : index + 1, :],
            )
            gram, drive = gram + more, drive + push
        set_weights(gram, jnp.broadcast_to(drive, gram.shape), mix, rest)

    groups, each, part = inner_ref.shape
    members = groups * each
    width = part // 4
    at = lax.broadcasted_iota(jnp.int32, (ROWS, members * 4), 0)
    slot = lax.broadcasted_iota(jnp.int32, (ROWS, members * 4), 1) // members
    mean = jnp.zeros((ROWS, width), jnp.float32)
    held = []
    for index, (part_ref, rows) in enumerate(((inner_ref, ROWS_INNER), (outer_ref, ROWS_OUTER))):
        flat = part_ref[...].reshape(members, part)
        stacked = jnp.concatenate([flat[:, i * width : (i + 1) * width] for i in range(4)], axis=0)
        source = jnp.zeros(at.shape, jnp.int32)
        for place, value in enumerate(rows):
            source = jnp.where(slot == place, value, source)
        ones = jnp.where(at == source, 1.0, 0.0).astype(jnp.bfloat16)
        mean = mean + jnp.dot(ones, stacked, preferred_element_type=jnp.float32)
        held.append(stacked)
    mean = mean * (1.0 / members)
    wide = 2 * LANES
    shape = (members // 2, ROWS, wide)
    home = is_inner(lax.broadcasted_iota(jnp.int32, shape, 1))
    rests = [jnp.concatenate([rest[i]] * (wide // LANES), axis=2) for i in range(2)]
    for start in range(0, width, wide):
        lanes = slice(start, start + wide)
        inner, outside = (
            jnp.dot(mix[i], held[i][:, lanes], preferred_element_type=jnp.float32).reshape(shape) for i in range(2)
        )
        low = jnp.where(home, inner, outside) + mean[None, :, lanes] * rests[0]
        high = pltpu.roll(jnp.where(home, outside, inner), 4, 1) + mean[None, :, lanes] * rests[1]
        half = (groups, PAIR, ROWS, wide)
        out_ref[:, 0:PAIR, 0, :, lanes] = low.reshape(half).astype(jnp.bfloat16)
        out_ref[:, PAIR : 2 * PAIR, 0, :, lanes] = high.reshape(half).astype(jnp.bfloat16)

def analyse(raw, south, north, obs, classes, inner, outer_part, levels, width):
    groups, each, _ = inner.shape
    members = groups * each
    half = pl.BlockSpec((groups, each, 4 * width), lambda i: (0, 0, i))
    small = [raw, south, north, obs, classes]
    return pl.pallas_call(
        analyse_kernel,
        grid=(levels,),
        in_specs=[pl.BlockSpec(a.shape, lambda i: (0, 0)) for a in small] + [half, half],
        out_specs=pl.BlockSpec((groups, each, 1, 8, width), lambda i: (0, 0, i, 0, 0)),
        out_shape=jax.ShapeDtypeStruct((groups, each, levels, 8, width), jnp.bfloat16),
        scratch_shapes=[
            pltpu.VMEM((2, members * ROWS // 2, members * 4), jnp.bfloat16),
            pltpu.VMEM((2, members // 2, ROWS, members), jnp.float32),
        ],
        compiler_params=params(LEAVE_ROOM),
        cost_estimate=cost(12),
        name="analyse",
    )(*small, inner, outer_part)


def to_neighbours(low, high):
    devices = lax.axis_size("space")
    up = [(i, i + 1) for i in range(devices - 1)]
    down = [(i + 1, i) for i in range(devices - 1)]
    return lax.ppermute(high, "space", up), lax.ppermute(low, "space", down)


def all_to_all(blocks):
    return lax.all_to_all(blocks, "member", split_axis=0, concat_axis=0, tiled=True)


def on_device(state, wind_east, wind_north, obs_col, obs_val, obs_rinv, obs_count, loc_class):
    members, tiles, levels, rows, width = state.shape
    slots = obs_col.shape[2]

    inner = interior(state, wind_east, wind_north)
    inner, state, wind_east, wind_north, obs_val, obs_rinv = lax.optimization_barrier(
        (inner, state, wind_east, wind_north, obs_val, obs_rinv)
    )
    inner_tile = all_to_all(inner)

    low, high = edge_rows(state)
    below, above = to_neighbours(low, high)
    winds = jnp.stack([wind_east[:, :, 0], wind_north[:, :, 0], wind_east[:, :, rows - 1], wind_north[:, :, rows - 1]])
    winds = jnp.swapaxes(winds, 1, 2)
    wind_below, wind_above = to_neighbours(winds[0:2], winds[2:4])
    live = jnp.arange(slots, dtype=jnp.int32) < obs_count[0, 0]
    obs = jnp.stack([obs_val[0, 0], jnp.where(live, obs_rinv[0, 0], jnp.float32(0.0))])
    obs_south, obs_north = to_neighbours(obs, obs)
    outside = outer(state, wind_east, wind_north, below, above, wind_below, wind_above)

    columns = obs_col[0]
    row = (columns // width) % rows
    inside = (row >= 2) & (row < rows - 2)
    kept = jnp.where(inside, row - 2, jnp.where(row < 2, row, row - 4))
    offset = (columns // (rows * width)) * (4 * width) + kept * width + columns % width
    span = 2 * LANES
    place, lane = offset // span, offset % span

    all_obs = jnp.concatenate([obs, obs_south, obs_north])
    outside, all_obs, inner_tile = lax.optimization_barrier((outside, all_obs, inner_tile))
    outer_tile = all_to_all(outside)
    raw = pick(jnp.where(inside, place, -1), lane, inner_tile, span)
    raw = pick(jnp.where(inside, -1, place), lane, outer_tile, span, raw)
    south, north = to_neighbours(raw, raw)
    updated = analyse(raw, south, north, all_obs, loc_class[0, 0], inner_tile, outer_tile, levels, width)
    final = all_to_all(updated)
    return jnp.swapaxes(final, 0, 1)


def solution(mesh):
    return jax.shard_map(
        on_device,
        mesh=mesh,
        in_specs=(
            P("member", None, None, "space", None),
            P(None, None, "space", None),
            P(None, None, "space", None),
            P("space", "member", None),
            P("space", "member", None),
            P("space", "member", None),
            P("space", "member"),
            P("space", "member", None, None),
        ),
        out_specs=P("member", None, None, "space", None),
        check_vma=False,
    )
```
